256 devices in a mesh: section: 2 (over z_hi), grp: 16 (over z_lo, y), sta: 8 (over x, core).
Axes of the slice: x: 4, y: 4, z: 8 (z_hi: 2, z_lo: 4; z = z_hi * 4 + z_lo), core: 2. Of those that a mesh axis runs over, the one named last changes fastest.
Arguments:
- records: bfloat16 [512, 4, 3, 16384], P(('section', 'grp', 'sta')), may hold values from -6 to 6
- fir_taps: float32 [64], replicated, may hold values from -0.75 to 0.75
- band_bins: int32 [4, 2], replicated, may hold values from 0 to 2048, as said below
- station_live: int32 [512], P(('section', 'grp', 'sta')), may hold values 0 or 1
- block_live: int32 [64], P(('section', 'grp')), may hold values 0 or 1
Outputs:
- correlations: float32 [2304, 64, 1024], P('sta', ('section', 'grp'))
The draws below stay inside these ranges and needn't reach their ends.
Inputs may be any that keep to these rules, and one draw needn't show every extreme that they name: band_bins[b, 0] < band_bins[b, 1]; each band spans 64 to 256 bins.
All inputs are finite; a program needn't handle non-finite values. No bound on the sum of `station_live` or of `block_live` on one device may be relied on, other than what follows from the above.
Results may differ from the reference program's by a relative error of at most 0.0077.
Values may be sent and summed in bfloat16 or wider, within the bound.
A program may use at most 64 MiB of HBM per device.

```python
import math
import jax
import jax.numpy as jnp
import numpy as np
from jax import lax

GROUP = 16
BINS = 2048
NT = 4096
DEC = 4
RAW = 16384
TAPS = 64
NBANDS = 4
BAND_MIN = 64
BAND_MAX = 256
SEG = 4
OFFS = 2
LAGS = 1024
GROUPS = 32
STATIONS = 512
BLOCKS = 64


def draw_band_bins(key, part):
    key = jax.random.fold_in(key, 11)
    subkeys = jax.random.split(key, 2)
    widths = jax.random.randint(subkeys[0], (NBANDS,), BAND_MIN, BAND_MAX + 1)
    widths = widths.at[0].set(BAND_MAX).at[NBANDS - 1].set(BAND_MIN)
    headroom = BINS - widths + 1
    starts = jax.random.randint(subkeys[1], (NBANDS,), 0, headroom)
    starts = starts.at[0].set(0).at[NBANDS - 1].set(BINS - BAND_MIN)
    return jnp.stack([starts, starts + widths], axis=1).astype(jnp.int32)


def set_ends(array, rng, smallest, top_value):
    longest = array.shape.index(max(array.shape))
    spots = []
    for shift in (0, 1):
        where = [jax.random.randint(jax.random.fold_in(rng, axis), (), 0, length) for axis, length in enumerate(array.shape)]
        where[longest] = (where[longest] + shift) % array.shape[longest]
        spots.append(tuple(where))
    return array.at[spots[0]].set(smallest).at[spots[1]].set(top_value)


def levels(stream_key, extent, cuts, low, high):
    def one(axis_at, shards_of):
        draws = jax.random.uniform(jax.random.fold_in(jax.random.fold_in(stream_key, 6), axis_at), (shards_of,), jnp.float32, low / len(cuts), high / len(cuts))
        return jnp.repeat(jnp.exp(draws), extent[axis_at] // shards_of).reshape((-1,) + (1,) * (len(extent) - axis_at - 1))

    level = one(*cuts[0])
    for cut in cuts[1:]:
        level = level * one(*cut)
    return level


def noise(own_key, extent, width, reach, cuts=(), kind=jnp.bfloat16):
    loudness = levels(own_key, extent, cuts, -0.22, 0.18) if cuts else 1.0
    entries = jax.random.normal(own_key, extent, jnp.float32) * width * loudness
    return jnp.minimum(jnp.maximum(entries, -reach), reach).astype(kind)


def setup_inputs(seed: int = 0) -> dict:
    keys = jax.random.split(jax.random.key(seed), 6)
    return {
        "records": noise(keys[0], (STATIONS, SEG, 3, RAW), 1.0, 6.0, ((0, 256),)),
        "fir_taps": noise(keys[1], (TAPS,), 0.125, 0.75, (), jnp.float32),
        "band_bins": draw_band_bins(jax.random.fold_in(keys[5], 71), 0),
        "station_live": set_ends((jax.random.randint(keys[3], (STATIONS,), 0, 8) < 7).astype(jnp.int32), jax.random.fold_in(keys[3], 1), 0, 1),
        "block_live": set_ends((jax.random.randint(keys[4], (BLOCKS,), 0, 4) < 3).astype(jnp.int32), jax.random.fold_in(keys[4], 1), 0, 1),
    }


epsilon = 1e-06

def decimate(recorded, fir_taps):
    signal = recorded.astype(jnp.float32)
    leading = signal.shape[:-1]
    lead_frames = TAPS // DEC + 1
    phases = jnp.swapaxes(signal.reshape(leading + (NT, DEC)), -1, -2)
    phases = jnp.pad(phases, [(0, 0)] * (len(leading) + 1) + [(lead_frames, 0)])
    summed = jnp.zeros(leading + (NT,), jnp.float32)
    for shift_back in range(lead_frames):
        tap_index = DEC * shift_back - np.arange(DEC)
        usable = (tap_index >= 0) & (tap_index < TAPS)
        coefficients = jnp.where(jnp.asarray(usable), fir_taps[np.clip(tap_index, 0, TAPS - 1)], 0.0)
        window = phases[..., lead_frames - shift_back:lead_frames - shift_back + NT]
        summed = summed + lax.optimization_barrier(jnp.sum(window * coefficients[:, None], axis=-2))
    return summed.astype(jnp.bfloat16)

def dft_table(starts, block_width):
    samples = jnp.arange(NT, dtype=jnp.int32)[:, None]
    bin_index = starts + jnp.arange(block_width, dtype=jnp.int32)[None, :]
    angles = 2.0 * math.pi / NT * (samples * bin_index % NT).astype(jnp.float32)
    return jnp.concatenate([jnp.cos(angles), -jnp.sin(angles)], axis=1).astype(jnp.bfloat16)

def whiten(real_part, imag_part, band_bins, station_live):
    bin_index = jnp.arange(BINS, dtype=jnp.int32)[None, :]
    inside = ((bin_index >= band_bins[:, 0:1]) & (bin_index < band_bins[:, 1:2])).astype(jnp.float32)
    band_width = (band_bins[:, 1] - band_bins[:, 0]).astype(jnp.float32)
    powers = (real_part * real_part + imag_part * imag_part).reshape(-1, BINS)
    energy = jnp.dot(powers, inside.T, precision=lax.Precision.HIGHEST) / band_width
    gains = jnp.dot(lax.rsqrt(energy + epsilon), inside, precision=lax.Precision.HIGHEST)
    gains = gains.reshape(real_part.shape) * station_live.astype(jnp.float32)[:, None, None, None]
    return jnp.concatenate([real_part * gains, imag_part * gains], axis=2).astype(jnp.bfloat16)

def cross_spectra(local_group, remote_group):
    local_re = local_group[:, :, :3].astype(jnp.float32)
    local_im = local_group[:, :, 3:].astype(jnp.float32)
    remote_re = remote_group[:, :, :3].astype(jnp.float32)
    remote_im = remote_group[:, :, 3:].astype(jnp.float32)
    real_sum = jnp.einsum('isaf,jsbf->iajbf', local_re, remote_re) + jnp.einsum('isaf,jsbf->iajbf', local_im, remote_im)
    imag_sum = jnp.einsum('isaf,jsbf->iajbf', local_im, remote_re) - jnp.einsum('isaf,jsbf->iajbf', local_re, remote_im)
    row_count = local_group.shape[0] * 9 * remote_group.shape[0]
    return jnp.concatenate([real_sum.reshape(row_count, -1), imag_sum.reshape(row_count, -1)], axis=1).astype(jnp.bfloat16)

def lag_table(frequency, parity, starts, block_width):
    lag_index = starts + jnp.arange(block_width, dtype=jnp.int32)[None, :] - LAGS // 2
    angles = 2.0 * math.pi / NT * (frequency[:, None] * lag_index % NT).astype(jnp.float32)
    weight = jnp.where(frequency == 0, 0.5, 1.0) / math.sqrt(BINS)
    values = jnp.where(parity[:, None] == 0, jnp.cos(angles), -jnp.sin(angles)) * weight[:, None]
    return values.astype(jnp.bfloat16)

def reference(records, fir_taps, band_bins, station_live, block_live):
    decimated = decimate(records, fir_taps)
    flattened = decimated.reshape(-1, NT)
    product = jnp.dot(flattened, dft_table(0, BINS), preferred_element_type=jnp.float32)
    out_shape = decimated.shape[:-1] + (BINS,)
    real_part = product[:, :BINS].reshape(out_shape)
    imag_part = product[:, BINS:].reshape(out_shape)
    whitened = whiten(real_part, imag_part, band_bins, station_live)
    groups = whitened.reshape(GROUPS, GROUP, SEG, 6, BINS)
    positions = jnp.arange(2 * BINS, dtype=jnp.int32)
    lag_weights = lag_table(positions % BINS, positions // BINS, 0, LAGS)

    def one_block(block_index):
        row_index = block_index // OFFS
        distance = block_index % OFFS + 1
        remote_index = (row_index - distance) % GROUPS
        local_group = lax.dynamic_index_in_dim(groups, row_index, 0, keepdims=False)
        remote_group = lax.dynamic_index_in_dim(groups, remote_index, 0, keepdims=False)
        spectra = cross_spectra(local_group, remote_group)
        kept = block_live[block_index].astype(jnp.float32)
        return jnp.dot(spectra, lag_weights, preferred_element_type=jnp.float32) * kept
    blocks_out = lax.map(one_block, jnp.arange(BLOCKS, dtype=jnp.int32))
    return jnp.transpose(blocks_out, (1, 0, 2))
```

```python
import functools
import math

import jax
import jax.numpy as jnp
import numpy as np
from jax import lax
from jax.experimental import pallas as pl
from jax.experimental.pallas import tpu as pltpu
from jax.sharding import PartitionSpec as P

BINS = 2048
NT = 4096
DEC = 4
TAPS = 64
OFFS = 2
LAGS = 1024
ROWS = 24
PADROWS = 32
FRAMES = 128
SPLIT = 32
WINDOW = 640
GROUPSLOTS = 32
TILES = 8
MESH = pl.DeviceIdType.MESH
VMEM_LIMIT = 56 * 1024 * 1024
HIGHEST = lax.Precision.HIGHEST


def constant_tables():
    i = np.arange(128)
    k = np.arange(32)[:, None]
    turn = 2.0 * np.pi / 4096
    twiddle = np.concatenate([np.cos(turn * k * i), -np.sin(turn * k * i)], 0).astype(np.float32)
    q = np.arange(64)
    fine = 2.0 * np.pi / 128 * (i[:, None] * q[None, :] % 128)
    second = np.concatenate([np.cos(fine), np.sin(fine)], 0).astype(np.float32)
    lag = np.arange(1024) - 512
    slow = turn * (k * lag[None, :] % 4096)
    lag_slow = np.concatenate([np.cos(slow), np.sin(slow)], 0).astype(np.float32)
    quick = np.zeros((128, 256))
    angle = 2.0 * np.pi / 128 * (q[:, None] * i[None, :] % 128)
    quick[:64, :128] = np.cos(angle)
    quick[:64, 128:] = np.sin(angle)
    return twiddle, second, lag_slow, quick.astype(np.float32)


def real_fft(values):
    n = len(values)
    if n == 2:
        return [(values[0] + values[1], None), (values[0] - values[1], None)]
    even = real_fft(values[0::2])
    odd = real_fft(values[1::2])
    result = [None] * (n // 2 + 1)
    for k in range(n // 4 + 1):
        er, ei = even[k]
        orr, oi = odd[k]
        c, s = math.cos(2 * math.pi * k / n), math.sin(2 * math.pi * k / n)
        if k == 0:
            tr, ti = orr, oi
        elif 4 * k == n:
            tr, ti = oi, -orr
        elif oi is None:
            tr, ti = orr * c, orr * (-s)
        else:
            tr, ti = orr * c + oi * s, oi * c - orr * s
        def plus(a, b):
            return b if a is None else a if b is None else a + b
        def minus(a, b):
            return (None if b is None else -b) if a is None else a if b is None else a - b
        result[k] = (plus(er, tr), plus(ei, ti))
        if n // 2 - k != k:
            low = minus(ti, ei)
            result[n // 2 - k] = (minus(er, tr), low)
    return result


def spectra_kernel(bands, live, taps, x_ref, tw_ref, second_ref, out_ref, band_scr, lhs1, dec, lhs2, wide, w2):
    f32, bf16 = jnp.float32, jnp.bfloat16
    a_index = lax.broadcasted_iota(jnp.int32, (WINDOW // 4, FRAMES), 0)
    o_index = lax.broadcasted_iota(jnp.int32, (WINDOW // 4, FRAMES), 1)
    lead = o_index - a_index + 32
    pieces = [jnp.zeros((WINDOW // 4, FRAMES), f32)] * 4
    for d in range(17):
        here = lead == d
        for b in range(4):
            if 0 <= 4 * d - b < 64:
                pieces[b] = jnp.where(here, taps[4 * d - b], pieces[b])
    for b in range(4):
        band_scr[pl.ds(b, WINDOW // 4, stride=4), :] = pieces[b]
    band = band_scr[...]
    high = band.astype(bf16)
    low = (band - high.astype(f32)).astype(bf16)
    weights = jnp.concatenate([high, low], axis=1)

    for j in range(SPLIT):
        rows = pl.ds(PADROWS * j, PADROWS)
        if j == 0:
            lhs1[rows, 0:128] = jnp.zeros((PADROWS, 128), bf16)
            lhs1[rows, 128:] = x_ref[:, 0:512]
        else:
            lhs1[rows, :] = x_ref[:, 512 * j - 128:512 * j + 512]
    summed = jnp.dot(lhs1[...], weights, preferred_element_type=f32)
    dec[...] = (summed[:, :128] + summed[:, 128:]).astype(bf16).astype(f32)

    q = lax.broadcasted_iota(jnp.int32, (64, 128), 0)
    lane = lax.broadcasted_iota(jnp.int32, (64, 128), 1)
    used = jnp.zeros((64, 128), jnp.bool_)
    for b in range(4):
        used = used | ((bands[0, b] < 32 * q + 32) & (bands[1, b] > 32 * q))
    usedf = jnp.where(used, 1.0, 0.0).astype(f32)
    q64 = lax.broadcasted_iota(jnp.int32, (64, 64), 0)
    p64 = lax.broadcasted_iota(jnp.int32, (64, 64), 1)
    before = jnp.where(p64 < q64, 1.0, 0.0).astype(f32)
    rank = jnp.dot(before, usedf, preferred_element_type=f32)
    pick = used & (rank == (lane % GROUPSLOTS).astype(f32))
    pickf = jnp.where(pick, 1.0, 0.0).astype(f32)
    group = jnp.sum(pickf * q.astype(f32), axis=0, keepdims=True)
    chosen = jnp.dot(second_ref[...].astype(bf16), pickf.astype(bf16), preferred_element_type=f32)
    cos_all, sin_all = chosen[:128], chosen[128:]
    lane128 = lax.broadcasted_iota(jnp.int32, (128, 128), 1)
    for kk in range(4):
        mine = lane128 // GROUPSLOTS == kk
        c = jnp.where(mine, cos_all, 0.0).astype(bf16)
        s = jnp.where(mine, sin_all, 0.0)
        w2[pl.ds(256 * kk, 128), 0:128] = c
        w2[pl.ds(256 * kk, 128), 128:256] = (-s).astype(bf16)
        w2[pl.ds(256 * kk + 128, 128), 0:128] = s.astype(bf16)
        w2[pl.ds(256 * kk + 128, 128), 128:256] = c

    def transform(chunk, carry):
        values = [dec[pl.ds(PADROWS * j + 8 * chunk, 8), :] for j in range(SPLIT)]
        freq = real_fft(values)
        for k1 in range(32):
            ar, ai = freq[k1] if k1 <= 16 else freq[32 - k1]
            c = tw_ref[pl.ds(k1, 1), :]
            s = tw_ref[pl.ds(32 + k1, 1), :]
            if ai is None:
                br, bi = ar * c, ar * s
            elif k1 <= 16:
                br, bi = ar * c - ai * s, ar * s + ai * c
            else:
                br, bi = ar * c + ai * s, ar * s - ai * c
            rows = pl.ds((k1 // 4) * ROWS + 8 * chunk, 8)
            column = (k1 % 4) * 256
            lhs2[rows, column:column + 128] = br
            lhs2[rows, column + 128:column + 256] = bi
        return carry

    lax.fori_loop(0, 3, transform, 0)
    y = jnp.dot(lhs2[...].astype(bf16), w2[...], preferred_element_type=f32)
    re, im = y[:, :128], y[:, 128:]
    power = re * re + im * im
    slot = lax.broadcasted_iota(jnp.int32, (1, 128), 1)
    bins = [4 * t + slot // GROUPSLOTS + 32 * group.astype(jnp.int32) for t in range(TILES)]
    gains = [jnp.zeros((ROWS, 128), f32)] * TILES
    station = lax.broadcasted_iota(jnp.int32, (ROWS, 1), 0)
    alive = jnp.where(station < 12, live[0].astype(f32), live[1].astype(f32))
    for b in range(4):
        total = jnp.zeros((ROWS, 128), f32)
        inside = []
        for t in range(TILES):
            m = (bins[t] >= bands[0, b]) & (bins[t] < bands[1, b])
            inside.append(m)
            total = total + jnp.where(m, power[ROWS * t:ROWS * t + ROWS], 0.0)
        width = (bands[1, b] - bands[0, b]).astype(f32)
        energy = jnp.sum(total, axis=1, keepdims=True) / width
        scale = lax.rsqrt(energy + 1e-06) * alive
        for t in range(TILES):
            gains[t] = gains[t] + jnp.where(inside[t], scale, 0.0)
    for t in range(TILES):
        rows = slice(ROWS * t, ROWS * t + ROWS)
        wre = re[rows] * gains[t]
        wim = im[rows] * gains[t]
        wide[pl.ds(t, ROWS, stride=16), :] = wre
        wide[pl.ds(8 + t, ROWS, stride=16), :] = wim
    out_ref[...] = wide[...].astype(bf16)


def smem():
    return pl.BlockSpec(memory_space=pltpu.SMEM)


def vmem():
    return pl.BlockSpec(memory_space=pltpu.VMEM)


def local_spectra(records, fir_taps, edges, station_live):
    twiddle, second, _, _ = constant_tables()
    x = jnp.transpose(records, (0, 2, 1, 3)).reshape(ROWS, -1)
    x = jnp.pad(x, ((0, PADROWS - ROWS), (0, 0)))
    f32, bf16 = jnp.float32, jnp.bfloat16
    return pl.pallas_call(
        spectra_kernel,
        out_shape=jax.ShapeDtypeStruct((ROWS * 16, 128), bf16),
        in_specs=[smem(), smem(), smem(), vmem(), vmem(), vmem()],
        out_specs=vmem(),
        scratch_shapes=[
            pltpu.VMEM((WINDOW, FRAMES), f32),
            pltpu.VMEM((PADROWS * SPLIT, WINDOW), bf16),
            pltpu.VMEM((PADROWS * SPLIT, FRAMES), f32),
            pltpu.VMEM((ROWS * TILES, 1024), f32),
            pltpu.VMEM((ROWS * 16, 128), f32),
            pltpu.VMEM((1024, 256), bf16),
        ],
        compiler_params=pltpu.CompilerParams(vmem_limit_bytes=VMEM_LIMIT),
        name="spectra",
    )(edges, station_live, fir_taps, x, twiddle, second)


def correlate_kernel(bands, kept, local_ref, remote_ref, slow_ref, quick_ref, out_ref, left, cross, lhs, table):
    f32, bf16 = jnp.float32, jnp.bfloat16
    left[...] = local_ref[...].astype(f32)

    def pairs(block, carry):
        k = block // 8
        s = block % 8
        for i2 in range(2):
            for b in range(3):
                rre, rim = [], []
                for w in range(4):
                    r = remote_ref[block, pl.ds((i2 * 12 + b * 4 + w) * 16, 16), :].astype(f32)
                    rre.append(r[0:8])
                    rim.append(r[8:16])
                for ia in range(6):
                    re = im = None
                    for w in range(4):
                        base = (ia * 4 + w) * 16
                        lre = left[base:base + 8, :]
                        lim = left[base + 8:base + 16, :]
                        pre = lre * rre[w] + lim * rim[w]
                        pim = lim * rre[w] - lre * rim[w]
                        re = pre if re is None else re + pre
                        im = pim if im is None else im + pim
                    row = k * 288 + ia * 48 + s * 6 + i2 * 3 + b
                    cross[pl.ds(row, 8, stride=1152), :] = re
                    cross[pl.ds(row + 576, 8, stride=1152), :] = im
        return carry

    lax.fori_loop(0, 16, pairs, 0)

    q = lax.broadcasted_iota(jnp.int32, (GROUPSLOTS, 128), 1)
    used = jnp.zeros((GROUPSLOTS, 128), jnp.bool_)
    for b in range(4):
        used = used | ((bands[0, b] < 32 * q + 32) & (bands[1, b] > 32 * q))
    used = used & (q < 64)
    usedf = jnp.where(used, 1.0, 0.0).astype(f32)
    p0 = lax.broadcasted_iota(jnp.int32, (128, 128), 0)
    p1 = lax.broadcasted_iota(jnp.int32, (128, 128), 1)
    before = jnp.where(p0 < p1, 1.0, 0.0).astype(f32)
    rank = jnp.dot(usedf, before, preferred_element_type=f32)
    g = lax.broadcasted_iota(jnp.int32, (GROUPSLOTS, 128), 0)
    pick = jnp.where(used & (rank == g.astype(f32)), 1.0, 0.0).astype(f32)
    quick = jnp.dot(pick, quick_ref[...], precision=HIGHEST, preferred_element_type=f32)
    quick = quick * f32(1.0 / math.sqrt(2048))
    qc, qs = quick[:, :128], quick[:, 128:]
    zero_bin = jnp.where((pick[:, 0:1] > 0.5), 0.5, 1.0)

    for t in range(TILES):
        for h in range(2):
            column = 256 * t + 128 * h
            lhs[:, column:column + 128] = cross[pl.ds(1152 * t + 576 * h, 576), :].astype(bf16)
        for kk in range(4):
            k1 = 4 * t + kk
            row = 256 * t + 32 * kk
            for n in range(8):
                lanes = slice(128 * n, 128 * n + 128)
                sc = slow_ref[pl.ds(k1, 1), lanes]
                ss = slow_ref[pl.ds(32 + k1, 1), lanes]
                wc = sc * qc - ss * qs
                ws = -(ss * qc + sc * qs)
                if k1 == 0:
                    wc, ws = wc * zero_bin, ws * zero_bin
                table[pl.ds(row, 32), lanes] = wc.astype(bf16)
                table[pl.ds(row + 128, 32), lanes] = ws.astype(bf16)
    for n in range(4):
        res = jnp.dot(lhs[...], table[:, 256 * n:256 * n + 256], preferred_element_type=f32)
        for k in range(2):
            part = res[288 * k:288 * k + 288] * kept[k].astype(f32)
            for h in range(2):
                out_ref[pl.ds((2 * n + h) * 2 + k, 288, stride=16), :] = part[:, 128 * h:128 * h + 128]


def correlate(local, remote, edges, block_live):
    _, _, slow, quick = constant_tables()
    f32, bf16 = jnp.float32, jnp.bfloat16
    out = pl.pallas_call(
        correlate_kernel,
        out_shape=jax.ShapeDtypeStruct((288 * 16, 128), f32),
        in_specs=[smem(), smem(), vmem(), vmem(), vmem(), vmem()],
        out_specs=vmem(),
        scratch_shapes=[
            pltpu.VMEM((ROWS * 16, 128), f32),
            pltpu.VMEM((1152 * TILES, 128), f32),
            pltpu.VMEM((576, 2048), bf16),
            pltpu.VMEM((2048, 1024), bf16),
        ],
        compiler_params=pltpu.CompilerParams(vmem_limit_bytes=VMEM_LIMIT),
        name="correlate",
    )(edges, block_live, local, remote, slow, quick)
    out = out.reshape(288, 8, 2, 128)
    return jnp.transpose(out, (0, 2, 1, 3)).reshape(288, 2, 1024)


def gather_kernel(parts, own_ref, out_ref, own_send, x_send, core_send, recv):
    section, grp, sta = lax.axis_index("section"), lax.axis_index("grp"), lax.axis_index("sta")
    groups = 16
    r = section * groups + grp
    mate = sta + 1 - 2 * lax.rem(sta, 2)
    peers = [lax.rem(sta + 2 * d, 8) for d in (1, 2, 3)]

    def at(shift):
        g = lax.rem(r + shift + 32, 32)
        return (g // groups, lax.rem(g, groups), sta)

    def near(s):
        return (section, grp, s)

    barrier = pltpu.get_barrier_semaphore()
    partners = [at(1), at(2), at(-1), at(-2), near(mate)] + [near(p) for p in peers]
    for who in partners:
        pl.semaphore_signal(barrier, inc=1, device_id=who, device_id_type=MESH)
    pl.semaphore_wait(barrier, len(partners))

    rows = own_ref.shape[0] // parts
    started = []

    def send(src, k, s, c, sem, who):
        copy = pltpu.make_async_remote_copy(
            src_ref=src,
            dst_ref=out_ref.at[k * 8 + s, pl.ds(c * rows, rows), :],
            send_sem=sem,
            recv_sem=recv.at[k * 8 + s, c],
            device_id=who,
            device_id_type=MESH,
        )
        copy.start()
        started.append(copy)

    def held(k, s, c):
        return out_ref.at[k * 8 + s, pl.ds(c * rows, rows), :]

    def arrived(k, s, c):
        pltpu.make_async_remote_copy(
            src_ref=held(k, s, c),
            dst_ref=held(k, s, c),
            send_sem=own_send.at[0, 0],
            recv_sem=recv.at[k * 8 + s, c],
            device_id=near(mate),
            device_id_type=MESH,
        ).wait_recv()

    for c in range(parts):
        for k in range(2):
            send(own_ref.at[pl.ds(c * rows, rows), :], k, sta, c, own_send.at[k, c], at(k + 1))
    for c in range(parts):
        for k in range(2):
            arrived(k, sta, c)
            for n, p in enumerate(peers):
                send(held(k, sta, c), k, sta, c, x_send.at[k, n, c], near(p))
            send(held(k, sta, c), k, sta, c, core_send.at[k, 0, c], near(mate))
    for c in range(parts):
        for k in range(2):
            for n, p in enumerate(peers):
                arrived(k, p, c)
                send(held(k, p, c), k, p, c, core_send.at[k, n + 1, c], near(mate))
    for c in range(parts):
        for k in range(2):
            for s in [mate] + [lax.rem(mate + 2 * d, 8) for d in (1, 2, 3)]:
                arrived(k, s, c)
    for copy in started:
        copy.wait_send()


def gather(local):
    parts = 2
    return pl.pallas_call(
        functools.partial(gather_kernel, parts),
        out_shape=jax.ShapeDtypeStruct((16,) + local.shape, local.dtype),
        in_specs=[vmem()],
        out_specs=vmem(),
        scratch_shapes=[
            pltpu.SemaphoreType.DMA((2, parts)),
            pltpu.SemaphoreType.DMA((2, 3, parts)),
            pltpu.SemaphoreType.DMA((2, 4, parts)),
            pltpu.SemaphoreType.DMA((16, parts)),
        ],
        compiler_params=pltpu.CompilerParams(collective_id=0, has_side_effects=True, vmem_limit_bytes=VMEM_LIMIT),
        name="gather",
    )(local)


def used_bins(records, fir_taps, band_bins, station_live, block_live):
    edges = jnp.transpose(band_bins)
    local = local_spectra(records, fir_taps, edges, station_live)
    return correlate(local, gather(local), edges, block_live)


def body(records, fir_taps, band_bins, station_live, block_live):
    q = jnp.arange(64, dtype=jnp.int32)[:, None]
    hit = (band_bins[None, :, 0] < 32 * q + 32) & (band_bins[None, :, 1] > 32 * q)
    count = jnp.sum(jnp.any(hit, axis=1).astype(jnp.int32))
    arguments = (records, fir_taps, band_bins, station_live, block_live)
    return lax.cond(count <= GROUPSLOTS, used_bins, every_bin, *arguments)


epsilon = 1e-06


def passed_along(block, axis, distance):
    devices = range(lax.axis_size(axis))
    route = [((i - distance) % len(devices), i) for i in devices]
    return lax.ppermute(block, axis, route)


def band_matrix(fir_taps, frames, offset):
    span = DEC * frames
    position = jnp.arange(span, dtype=jnp.int32)[:, None]
    output = jnp.arange(frames, dtype=jnp.int32)[None, :]
    tap_index = DEC * output + offset - position
    usable = (tap_index >= 0) & (tap_index < TAPS)
    return jnp.where(usable, fir_taps[jnp.clip(tap_index, 0, TAPS - 1)], 0.0)


def decimate(recorded, fir_taps):
    leading = recorded.shape[:-1]
    frames = min(NT, 128)
    span = DEC * frames
    block_count = NT // frames
    signal = recorded.astype(jnp.float32).reshape(-1, block_count, span)
    previous = jnp.pad(signal[:, :-1], ((0, 0), (1, 0), (0, 0)))
    current_part = jnp.dot(
        signal.reshape(-1, span), band_matrix(fir_taps, frames, 0), precision=lax.Precision.HIGHEST
    )
    previous_part = jnp.dot(
        previous.reshape(-1, span),
        band_matrix(fir_taps, frames, span),
        precision=lax.Precision.HIGHEST,
    )
    summed = current_part + previous_part
    return summed.reshape(leading + (NT,)).astype(jnp.bfloat16)


def dft_table(starts, block_width):
    samples = jnp.arange(NT, dtype=jnp.int32)[:, None]
    bin_index = starts + jnp.arange(block_width, dtype=jnp.int32)[None, :]
    angles = 2.0 * math.pi / NT * (samples * bin_index % NT).astype(jnp.float32)
    return jnp.concatenate([jnp.cos(angles), -jnp.sin(angles)], axis=1).astype(jnp.bfloat16)


def spectrum(flattened):
    block_width = min(BINS, 256)

    def spectrum_advance(loop_step, buffers):
        real_part, imag_part = buffers
        starts = loop_step * block_width
        product = jnp.dot(
            flattened, dft_table(starts, block_width), preferred_element_type=jnp.float32
        )
        real_part = lax.dynamic_update_slice_in_dim(real_part, product[:, :block_width], starts, 1)
        imag_part = lax.dynamic_update_slice_in_dim(imag_part, product[:, block_width:], starts, 1)
        return (real_part, imag_part)

    empty_buffer = jnp.zeros((flattened.shape[0], BINS), jnp.float32)
    return lax.fori_loop(0, BINS // block_width, spectrum_advance, (empty_buffer, empty_buffer))


def whiten(real_part, imag_part, band_bins, station_live):
    bin_index = jnp.arange(BINS, dtype=jnp.int32)[None, :]
    inside = ((bin_index >= band_bins[:, 0:1]) & (bin_index < band_bins[:, 1:2])).astype(
        jnp.float32
    )
    band_width = (band_bins[:, 1] - band_bins[:, 0]).astype(jnp.float32)
    powers = (real_part * real_part + imag_part * imag_part).reshape(-1, BINS)
    energy = jnp.dot(powers, inside.T, precision=lax.Precision.HIGHEST) / band_width
    gains = jnp.dot(lax.rsqrt(energy + epsilon), inside, precision=lax.Precision.HIGHEST)
    gains = gains.reshape(real_part.shape) * station_live.astype(jnp.float32)[:, None, None, None]
    return jnp.concatenate([real_part * gains, imag_part * gains], axis=2).astype(jnp.bfloat16)


def cross_spectra(local_group, remote_group):
    local_swap = jnp.swapaxes(local_group, 1, 2)
    remote_swap = jnp.swapaxes(remote_group, 1, 2)
    local_re = local_swap[:, :3, None, None].astype(jnp.float32)
    local_im = local_swap[:, 3:, None, None].astype(jnp.float32)
    remote_re = remote_swap[None, None, :, :3].astype(jnp.float32)
    remote_im = remote_swap[None, None, :, 3:].astype(jnp.float32)
    real_sum = jnp.sum(local_re * remote_re + local_im * remote_im, axis=4)
    imag_sum = jnp.sum(local_im * remote_re - local_re * remote_im, axis=4)
    row_count = local_group.shape[0] * 9 * remote_group.shape[0]
    return jnp.concatenate(
        [real_sum.reshape(row_count, -1), imag_sum.reshape(row_count, -1)], axis=1
    ).astype(jnp.bfloat16)


def lag_table(frequency, parity, starts, block_width):
    lag_index = starts + jnp.arange(block_width, dtype=jnp.int32)[None, :] - LAGS // 2
    angles = 2.0 * math.pi / NT * (frequency[:, None] * lag_index % NT).astype(jnp.float32)
    weight = jnp.where(frequency == 0, 0.5, 1.0) / math.sqrt(BINS)
    values = jnp.where(parity[:, None] == 0, jnp.cos(angles), -jnp.sin(angles)) * weight[:, None]
    return values.astype(jnp.bfloat16)


def inverse(spectra, frequency, parity, kept_blocks):
    row_count, block_count, depth = spectra.shape
    flattened = spectra.reshape(row_count * block_count, depth)
    block_width = min(LAGS, 256)

    def inverse_advance(loop_step, result):
        starts = loop_step * block_width
        product = jnp.dot(
            flattened,
            lag_table(frequency, parity, starts, block_width),
            preferred_element_type=jnp.float32,
        )
        return lax.dynamic_update_slice_in_dim(result, product, starts, 1)

    result = lax.fori_loop(
        0,
        LAGS // block_width,
        inverse_advance,
        jnp.zeros((row_count * block_count, LAGS), jnp.float32),
    )
    return result.reshape(row_count, block_count, LAGS) * kept_blocks[None, :, None]


def every_bin(records, fir_taps, band_bins, station_live, block_live):
    decimated = decimate(records, fir_taps)
    real_part, imag_part = spectrum(decimated.reshape(-1, NT))
    out_shape = decimated.shape[:-1] + (BINS,)
    local_spectra = whiten(
        real_part.reshape(out_shape), imag_part.reshape(out_shape), band_bins, station_live
    )
    kept_blocks = block_live.astype(jnp.float32)
    gathered = lax.all_gather(local_spectra, "sta", axis=0, tiled=True)
    remote = gathered
    pieces = []
    for distance in range(OFFS):
        remote = passed_along(remote, ("section", "grp"), 1)
        pieces.append(cross_spectra(local_spectra, remote))
    arrived = jnp.stack(pieces, axis=1)
    positions = jnp.arange(2 * BINS, dtype=jnp.int32)
    frequency = positions % BINS
    parity = positions // BINS
    return inverse(arrived, frequency, parity, kept_blocks)


def solution(mesh):
    in_specs = (
        P(("section", "grp", "sta"), None, None, None),
        P(),
        P(),
        P(("section", "grp", "sta")),
        P(("section", "grp")),
    )
    out_specs = P("sta", ("section", "grp"), None)
    return jax.shard_map(body, mesh=mesh, in_specs=in_specs, out_specs=out_specs, check_vma=False)
```

```python
import functools
import math

import jax
import jax.numpy as jnp
import numpy as np
from jax import lax
from jax.experimental import pallas as pl
from jax.experimental.pallas import tpu as pltpu
from jax.sharding import PartitionSpec as P

ROWS = 24
PADROWS = 32
FRAMES = 128
SPLIT = 32
WINDOW = 640
TILES = 8
MESH = pl.DeviceIdType.MESH
VMEM_LIMIT = 40 * 1024 * 1024
HIGHEST = lax.Precision.HIGHEST


def constant_tables():
    i = np.arange(128)
    k = np.arange(32)[:, None]
    turn = 2.0 * np.pi / 4096
    twiddle = np.concatenate([np.cos(turn * k * i), -np.sin(turn * k * i)], 0).astype(np.float32)
    q = np.arange(64)
    fine = 2.0 * np.pi / 128 * (i[:, None] * q[None, :] % 128)
    second = np.concatenate([np.cos(fine), np.sin(fine)], 0).astype(np.float32)
    lag = np.arange(1024) - 512
    slow = turn * (k * lag[None, :] % 4096)
    lag_slow = np.concatenate([np.cos(slow), np.sin(slow)], 0).astype(np.float32)
    quick = np.zeros((128, 256))
    angle = 2.0 * np.pi / 128 * (q[:, None] * i[None, :] % 128)
    quick[:64, :128] = np.cos(angle)
    quick[:64, 128:] = np.sin(angle)
    return twiddle, second, lag_slow, quick.astype(np.float32)


def real_fft(values):
    n = len(values)
    if n == 2:
        return [(values[0] + values[1], None), (values[0] - values[1], None)]
    even = real_fft(values[0::2])
    odd = real_fft(values[1::2])
    result = [None] * (n // 2 + 1)
    for k in range(n // 4 + 1):
        er, ei = even[k]
        orr, oi = odd[k]
        c, s = math.cos(2 * math.pi * k / n), math.sin(2 * math.pi * k / n)
        if k == 0:
            tr, ti = orr, oi
        elif 4 * k == n:
            tr, ti = oi, -orr
        elif oi is None:
            tr, ti = orr * c, orr * (-s)
        else:
            tr, ti = orr * c + oi * s, oi * c - orr * s
        def plus(a, b):
            return b if a is None else a if b is None else a + b
        def minus(a, b):
            return (None if b is None else -b) if a is None else a if b is None else a - b
        result[k] = (plus(er, tr), plus(ei, ti))
        if n // 2 - k != k:
            low = minus(ti, ei)
            result[n // 2 - k] = (minus(er, tr), low)
    return result


def filter_weights(taps, band_scr):
    f32, bf16 = jnp.float32, jnp.bfloat16
    a_index = lax.broadcasted_iota(jnp.int32, (WINDOW // 4, FRAMES), 0)
    o_index = lax.broadcasted_iota(jnp.int32, (WINDOW // 4, FRAMES), 1)
    lead = o_index - a_index + 32
    pieces = [jnp.zeros((WINDOW // 4, FRAMES), f32)] * 4
    for d in range(17):
        here = lead == d
        for b in range(4):
            if 0 <= 4 * d - b < 64:
                pieces[b] = jnp.where(here, taps[4 * d - b], pieces[b])
    for b in range(4):
        band_scr[pl.ds(b, WINDOW // 4, stride=4), :] = pieces[b]
    band = band_scr[...]
    high = band.astype(bf16)
    low = (band - high.astype(f32)).astype(bf16)
    return jnp.concatenate([high, low], axis=1)


def by_band(index, values):
    result = jnp.full(index.shape, values[3], jnp.int32)
    for b in range(3):
        result = jnp.where(index == b, values[b], result)
    return result


def band_edges(bands):
    first = [bands[0, b] for b in range(4)]
    last = [bands[1, b] for b in range(4)]
    return first, last, [s // 32 for s in first], [s % 32 for s in first]


def second_stage(bands, second_ref, w2):
    f32, bf16 = jnp.float32, jnp.bfloat16
    _, _, coarse, _ = band_edges(bands)
    q = lax.broadcasted_iota(jnp.int32, (64, 128), 0)
    lane = lax.broadcasted_iota(jnp.int32, (64, 128), 1)
    base = by_band(lane % 32 // 8, coarse) + lane % 8
    lane128 = lax.broadcasted_iota(jnp.int32, (128, 128), 1)
    for late in range(2):
        pick = jnp.where(q == base + late, 1.0, 0.0).astype(bf16)
        chosen = jnp.dot(second_ref[...].astype(bf16), pick, preferred_element_type=f32)
        for kk in range(4):
            mine = lane128 // 32 == kk
            c = jnp.where(mine, chosen[:128], 0.0)
            s = jnp.where(mine, chosen[128:], 0.0)
            top, under = pl.ds(256 * kk, 128), pl.ds(256 * kk + 128, 128)
            re, im = slice(256 * late, 256 * late + 128), slice(256 * late + 128, 256 * late + 256)
            w2[top, re] = c.astype(bf16)
            w2[top, im] = (-s).astype(bf16)
            w2[under, re] = s.astype(bf16)
            w2[under, im] = c.astype(bf16)


def transform(dec, tw_ref, lhs2):
    def one(chunk, carry):
        values = [dec[pl.ds(PADROWS * j + 8 * chunk, 8), :] for j in range(SPLIT)]
        freq = real_fft(values)
        for k1 in range(32):
            ar, ai = freq[k1] if k1 <= 16 else freq[32 - k1]
            c = tw_ref[pl.ds(k1, 1), :]
            s = tw_ref[pl.ds(32 + k1, 1), :]
            if ai is None:
                br, bi = ar * c, ar * s
            elif k1 <= 16:
                br, bi = ar * c - ai * s, ar * s + ai * c
            else:
                br, bi = ar * c + ai * s, ar * s - ai * c
            rows = pl.ds((k1 // 4) * ROWS + 8 * chunk, 8)
            column = (k1 % 4) * 256
            lhs2[rows, column:column + 128] = br
            lhs2[rows, column + 128:column + 256] = bi
        return carry

    lax.fori_loop(0, 3, one, 0)


def whiten_slots(bands, live, y, wide):
    f32 = jnp.float32
    first, last, coarse, fine = band_edges(bands)
    slot = lax.broadcasted_iota(jnp.int32, (1, 128), 1)
    owner = slot % 32 // 8
    base = by_band(owner, coarse) + slot % 8
    offset = by_band(owner, fine)
    re, im, inside, counted = [], [], [], []
    for t in range(TILES):
        k1 = 4 * t + slot // 32
        late = k1 < offset
        bins = k1 + 32 * (base + jnp.where(late, 1, 0))
        rows = slice(ROWS * t, ROWS * t + ROWS)
        re.append(jnp.where(late, y[rows, 256:384], y[rows, 0:128]))
        im.append(jnp.where(late, y[rows, 384:512], y[rows, 128:256]))
        within = [(bins >= first[b]) & (bins < last[b]) for b in range(4)]
        inside.append(within)
        own = within[0] & (owner == 0)
        for b in range(1, 4):
            mine = within[b] & (owner == b)
            for earlier in range(b):
                mine = mine & jnp.logical_not(within[earlier])
            own = own | mine
        counted.append(own)
    station = lax.broadcasted_iota(jnp.int32, (ROWS, 1), 0)
    alive = jnp.where(station < 12, live[0].astype(f32), live[1].astype(f32))
    gains = [jnp.zeros((ROWS, 128), f32)] * TILES
    for b in range(4):
        total = jnp.zeros((ROWS, 128), f32)
        for t in range(TILES):
            power = re[t] * re[t] + im[t] * im[t]
            total = total + jnp.where(inside[t][b] & (owner == b), power, 0.0)
        width = (last[b] - first[b]).astype(f32)
        energy = jnp.sum(total, axis=1, keepdims=True) / width
        scale = lax.rsqrt(energy + 1e-06) * alive
        for t in range(TILES):
            gains[t] = gains[t] + jnp.where(inside[t][b], scale, 0.0)
    for t in range(TILES):
        gain = jnp.where(counted[t], gains[t], 0.0)
        wide[pl.ds(t, ROWS, stride=16), :] = re[t] * gain
        wide[pl.ds(8 + t, ROWS, stride=16), :] = im[t] * gain


def lag_groups(bands, quick_ref):
    f32 = jnp.float32
    _, _, coarse, fine = band_edges(bands)
    g = lax.broadcasted_iota(jnp.int32, (32, 128), 0)
    q = lax.broadcasted_iota(jnp.int32, (32, 128), 1)
    base = by_band(g // 8, coarse) + g % 8
    offset = by_band(g // 8, fine)
    tables = []
    for late in range(2):
        pick = jnp.where(q == base + late, 1.0, 0.0).astype(f32)
        quick = jnp.dot(pick, quick_ref[...], precision=HIGHEST, preferred_element_type=f32)
        quick = quick * f32(1.0 / math.sqrt(2048))
        tables.append((quick[:, :128], quick[:, 128:]))
    return base, offset, tables


def lag_tile(t, base, offset, tables, slow_ref, table):
    bf16 = jnp.bfloat16
    for kk in range(4):
        k1 = 4 * t + kk
        late = k1 < offset
        qc = jnp.where(late, tables[1][0], tables[0][0])
        qs = jnp.where(late, tables[1][1], tables[0][1])
        if k1 == 0:
            half = jnp.where(base + jnp.where(late, 1, 0) == 0, 0.5, 1.0)
            qc, qs = qc * half, qs * half
        row = 256 * t + 32 * kk
        for n in range(8):
            lanes = slice(128 * n, 128 * n + 128)
            sc = slow_ref[pl.ds(k1, 1), lanes]
            ss = slow_ref[pl.ds(32 + k1, 1), lanes]
            table[pl.ds(row, 32), lanes] = (sc * qc - ss * qs).astype(bf16)
            table[pl.ds(row + 128, 32), lanes] = (-(ss * qc + sc * qs)).astype(bf16)


def cross_block(left, got, cross, k, s):
    f32 = jnp.float32
    for i2 in range(2):
        for b in range(3):
            rre, rim = [], []
            for w in range(4):
                r = got[k * 8 + s, pl.ds((i2 * 12 + b * 4 + w) * 16, 16), :].astype(f32)
                rre.append(r[0:8])
                rim.append(r[8:16])
            for ia in range(6):
                re = im = None
                for w in range(4):
                    at = (ia * 4 + w) * 16
                    lre = left[at:at + 8, :]
                    lim = left[at + 8:at + 16, :]
                    pre = lre * rre[w] + lim * rim[w]
                    pim = lim * rre[w] - lre * rim[w]
                    re = pre if re is None else re + pre
                    im = pim if im is None else im + pim
                row = k * 288 + ia * 48 + s * 6 + i2 * 3 + b
                cross[pl.ds(row, 8, stride=1152), :] = re
                cross[pl.ds(row + 576, 8, stride=1152), :] = im


def whole_kernel(parts, bands, live, taps, kept, x_any, tw_ref, second_ref, slow_ref, quick_ref, out_ref,
                 x_in, band_scr, lhs1, dec, lhs2, wide, w2, own_ref, got, cross, lhs, table,
                 x_sem, y_send, x_send, f_send, m_send, recv):
    f32, bf16 = jnp.float32, jnp.bfloat16
    section, grp, sta = lax.axis_index("section"), lax.axis_index("grp"), lax.axis_index("sta")
    groups = 16
    r = section * groups + grp
    mate = sta + 1 - 2 * lax.rem(sta, 2)
    right, across, left_peer = [lax.rem(sta + 2 * d, 8) for d in (1, 2, 3)]

    def group_at(shift):
        g = lax.rem(r + shift + 32, 32)
        return (g // groups, lax.rem(g, groups), sta)

    def near(s):
        return (section, grp, s)

    barrier = pltpu.get_barrier_semaphore()
    partners = [group_at(1), group_at(-1), near(mate), near(right), near(left_peer)]
    for who in partners:
        pl.semaphore_signal(barrier, inc=1, device_id=who, device_id_type=MESH)

    fetches = [pltpu.make_async_copy(x_any.at[n], x_in.at[n], x_sem.at[n]) for n in range(6)]
    for fetch in fetches:
        fetch.start()
    weights = filter_weights(taps, band_scr)
    second_stage(bands, second_ref, w2)
    for fetch in fetches:
        fetch.wait()
    x = x_in[...].reshape(ROWS, -1)
    x = jnp.concatenate([x, jnp.zeros((PADROWS - ROWS, x.shape[1]), bf16)], axis=0)
    for j in range(SPLIT):
        rows = pl.ds(PADROWS * j, PADROWS)
        if j == 0:
            lhs1[rows, 0:128] = jnp.zeros((PADROWS, 128), bf16)
            lhs1[rows, 128:] = x[:, 0:512]
        else:
            lhs1[rows, :] = x[:, 512 * j - 128:512 * j + 512]
    summed = jnp.dot(lhs1[...], weights, preferred_element_type=f32)
    dec[...] = (summed[:, :128] + summed[:, 128:]).astype(bf16).astype(f32)
    transform(dec, tw_ref, lhs2)
    y = jnp.dot(lhs2[...].astype(bf16), w2[...], preferred_element_type=f32)
    whiten_slots(bands, live, y, wide)
    own_ref[...] = wide[...].astype(bf16)

    pl.semaphore_wait(barrier, len(partners))
    rows = own_ref.shape[0] // parts
    started = []

    def held(k, s, c):
        return got.at[k * 8 + s, pl.ds(c * rows, rows), :]

    def send(src, k, s, c, sem, who):
        copy = pltpu.make_async_remote_copy(
            src_ref=src, dst_ref=held(k, s, c), send_sem=sem, recv_sem=recv.at[k * 8 + s, c],
            device_id=who, device_id_type=MESH,
        )
        copy.start()
        started.append(copy)

    def arrived(k, s, c):
        pltpu.make_async_remote_copy(
            src_ref=held(k, s, c), dst_ref=held(k, s, c), send_sem=y_send.at[0, 0],
            recv_sem=recv.at[k * 8 + s, c], device_id=near(mate), device_id_type=MESH,
        ).wait_recv()

    def own_column(k, c):
        arrived(k, sta, c)
        if k == 0:
            send(held(0, sta, c), 1, sta, c, y_send.at[1, c], group_at(1))
        send(held(k, sta, c), k, sta, c, x_send.at[k, 0, c], near(right))
        send(held(k, sta, c), k, sta, c, x_send.at[k, 1, c], near(left_peer))
        send(held(k, sta, c), k, sta, c, m_send.at[k, 0, c], near(mate))

    def from_left(k, c):
        arrived(k, left_peer, c)
        if 2 * c < parts:
            send(held(k, left_peer, c), k, left_peer, c, f_send.at[k, c], near(right))
        send(held(k, left_peer, c), k, left_peer, c, m_send.at[k, 1, c], near(mate))

    def from_right(k, c):
        arrived(k, right, c)
        if 2 * c >= parts:
            send(held(k, right, c), k, right, c, f_send.at[k, c], near(left_peer))
        send(held(k, right, c), k, right, c, m_send.at[k, 2, c], near(mate))

    def from_across(k, c):
        arrived(k, across, c)
        send(held(k, across, c), k, across, c, m_send.at[k, 3, c], near(mate))

    def sides(k):
        for c in range(parts):
            from_left(k, c)
            from_right(k, parts - 1 - c)

    def far(k):
        for c in range(parts // 2):
            from_across(k, c)
            from_across(k, parts // 2 + c)

    def by_mate(k, s):
        for c in range(parts):
            arrived(k, s, c)

    def several(k, start, count):
        def one(n, carry):
            cross_block(wide, got, cross, k, lax.rem(start + 2 * n, 8))
            return carry
        lax.fori_loop(0, count, one, 0)

    def pack(k):
        rows = pl.ds(288 * k, 288)
        for t in range(TILES):
            for h in range(2):
                column = 256 * t + 128 * h
                lhs[rows, column:column + 128] = cross[pl.ds(1152 * t + 576 * h + 288 * k, 288), :].astype(bf16)

    def product(k, n):
        part = jnp.dot(lhs[pl.ds(288 * k, 288), :], table[:, 256 * n:256 * n + 256], preferred_element_type=f32)
        part = part * kept[k].astype(f32)
        for h in range(2):
            out_ref[pl.ds((2 * n + h) * 2 + k, 288, stride=16), :] = part[:, 128 * h:128 * h + 128]

    for c in range(parts):
        send(own_ref.at[pl.ds(c * rows, rows), :], 0, sta, c, y_send.at[0, c], group_at(1))
    base, offset, tables = lag_groups(bands, quick_ref)
    for c in range(parts):
        own_column(0, c)
    for t in range(4):
        lag_tile(t, base, offset, tables, slow_ref, table)
    for c in range(parts):
        own_column(1, c)
    sides(0)
    for t in range(4, 8):
        lag_tile(t, base, offset, tables, slow_ref, table)
    far(0)
    several(0, sta, 1)
    sides(1)
    several(0, lax.rem(sta + 2, 8), 3)
    for d in range(4):
        by_mate(0, lax.rem(mate + 2 * d, 8))
    far(1)
    several(0, mate, 4)
    pack(0)
    for n in range(4):
        product(0, n)
    several(1, sta, 4)
    for d in range(4):
        by_mate(1, lax.rem(mate + 2 * d, 8))
    several(1, mate, 4)
    pack(1)
    for n in range(4):
        product(1, n)
    for copy in started:
        copy.wait_send()


def smem():
    return pl.BlockSpec(memory_space=pltpu.SMEM)


def vmem():
    return pl.BlockSpec(memory_space=pltpu.VMEM)


def body(records, fir_taps, band_bins, station_live, block_live):
    twiddle, second, slow, quick = constant_tables()
    f32, bf16 = jnp.float32, jnp.bfloat16
    x = jnp.transpose(records, (0, 2, 1, 3)).reshape(6, 4, -1)
    parts = 2
    dma = pltpu.SemaphoreType.DMA
    out = pl.pallas_call(
        functools.partial(whole_kernel, parts),
        out_shape=jax.ShapeDtypeStruct((288 * 16, 128), f32),
        in_specs=[smem(), smem(), smem(), smem(), pl.BlockSpec(memory_space=pl.ANY), vmem(), vmem(), vmem(), vmem()],
        out_specs=vmem(),
        scratch_shapes=[
            pltpu.VMEM((6, 4, 16384), bf16),
            pltpu.VMEM((WINDOW, FRAMES), f32),
            pltpu.VMEM((PADROWS * SPLIT, WINDOW), bf16),
            pltpu.VMEM((PADROWS * SPLIT, FRAMES), f32),
            pltpu.VMEM((ROWS * TILES, 1024), f32),
            pltpu.VMEM((ROWS * 16, 128), f32),
            pltpu.VMEM((1024, 512), bf16),
            pltpu.VMEM((ROWS * 16, 128), bf16),
            pltpu.VMEM((16, ROWS * 16, 128), bf16),
            pltpu.VMEM((1152 * TILES, 128), f32),
            pltpu.VMEM((576, 2048), bf16),
            pltpu.VMEM((2048, 1024), bf16),
            dma((6,)),
            dma((2, parts)),
            dma((2, 2, parts)),
            dma((2, parts)),
            dma((2, 4, parts)),
            dma((16, parts)),
        ],
        compiler_params=pltpu.CompilerParams(collective_id=0, has_side_effects=True, vmem_limit_bytes=VMEM_LIMIT),
        name="whole",
    )(jnp.transpose(band_bins), station_live, fir_taps, block_live, x, twiddle, second, slow, quick)
    out = out.reshape(288, 8, 2, 128)
    return jnp.transpose(out, (0, 2, 1, 3)).reshape(288, 2, 1024)


def solution(mesh):
    in_specs = (
        P(("section", "grp", "sta"), None, None, None),
        P(),
        P(),
        P(("section", "grp", "sta")),
        P(("section", "grp")),
    )
    out_specs = P("sta", ("section", "grp"), None)
    return jax.shard_map(body, mesh=mesh, in_specs=in_specs, out_specs=out_specs, check_vma=False)
```

```python
import functools
import math

import jax
import jax.numpy as jnp
import numpy as np
from jax import lax
from jax.experimental import pallas as pl
from jax.experimental.pallas import tpu as pltpu
from jax.sharding import PartitionSpec as P

ROWS = 24
PADROWS = 32
FRAMES = 128
SPLIT = 32
WINDOW = 640
TILES = 8
MESH = pl.DeviceIdType.MESH
VMEM_LIMIT = 40 * 1024 * 1024
HIGHEST = lax.Precision.HIGHEST


def constant_tables():
    i = np.arange(128)
    k = np.arange(32)[:, None]
    turn = 2.0 * np.pi / 4096
    twiddle = np.concatenate([np.cos(turn * k * i), -np.sin(turn * k * i)], 0).astype(np.float32)
    q = np.arange(64)
    fine = 2.0 * np.pi / 128 * (i[:, None] * q[None, :] % 128)
    second = np.concatenate([np.cos(fine), np.sin(fine)], 0).astype(np.float32)
    lag = np.arange(1024) - 512
    slow = turn * (k * lag[None, :] % 4096)
    lag_slow = np.concatenate([np.cos(slow), np.sin(slow)], 0).astype(np.float32)
    quick = np.zeros((128, 256))
    angle = 2.0 * np.pi / 128 * (q[:, None] * i[None, :] % 128)
    quick[:64, :128] = np.cos(angle)
    quick[:64, 128:] = np.sin(angle)
    return twiddle, second, lag_slow, quick.astype(np.float32)


def real_fft(values):
    n = len(values)
    if n == 2:
        return [(values[0] + values[1], None), (values[0] - values[1], None)]
    even = real_fft(values[0::2])
    odd = real_fft(values[1::2])
    result = [None] * (n // 2 + 1)
    for k in range(n // 4 + 1):
        er, ei = even[k]
        orr, oi = odd[k]
        c, s = math.cos(2 * math.pi * k / n), math.sin(2 * math.pi * k / n)
        if k == 0:
            tr, ti = orr, oi
        elif 4 * k == n:
            tr, ti = oi, -orr
        elif oi is None:
            tr, ti = orr * c, orr * (-s)
        else:
            tr, ti = orr * c + oi * s, oi * c - orr * s
        def plus(a, b):
            return b if a is None else a if b is None else a + b
        def minus(a, b):
            return (None if b is None else -b) if a is None else a if b is None else a - b
        result[k] = (plus(er, tr), plus(ei, ti))
        if n // 2 - k != k:
            low = minus(ti, ei)
            result[n // 2 - k] = (minus(er, tr), low)
    return result


def filter_weights(taps, band_scr):
    f32, bf16 = jnp.float32, jnp.bfloat16
    a_index = lax.broadcasted_iota(jnp.int32, (WINDOW // 4, FRAMES), 0)
    o_index = lax.broadcasted_iota(jnp.int32, (WINDOW // 4, FRAMES), 1)
    lead = o_index - a_index + 32
    pieces = [jnp.zeros((WINDOW // 4, FRAMES), f32)] * 4
    for d in range(17):
        here = lead == d
        for b in range(4):
            if 0 <= 4 * d - b < 64:
                pieces[b] = jnp.where(here, taps[4 * d - b], pieces[b])
    for b in range(4):
        band_scr[pl.ds(b, WINDOW // 4, stride=4), :] = pieces[b]
    band = band_scr[...]
    high = band.astype(bf16)
    low = (band - high.astype(f32)).astype(bf16)
    return jnp.concatenate([high, low], axis=1)


def by_band(index, values):
    result = jnp.full(index.shape, values[3], jnp.int32)
    for b in range(3):
        result = jnp.where(index == b, values[b], result)
    return result


def band_edges(bands):
    first = [bands[0, b] for b in range(4)]
    last = [bands[1, b] for b in range(4)]
    return first, last, [s // 32 for s in first], [s % 32 for s in first]


def second_stage(bands, second_ref, w2):
    f32, bf16 = jnp.float32, jnp.bfloat16
    _, _, coarse, _ = band_edges(bands)
    q = lax.broadcasted_iota(jnp.int32, (64, 128), 0)
    lane = lax.broadcasted_iota(jnp.int32, (64, 128), 1)
    base = by_band(lane % 32 // 8, coarse) + lane % 8
    lane128 = lax.broadcasted_iota(jnp.int32, (128, 128), 1)
    for late in range(2):
        pick = jnp.where(q == base + late, 1.0, 0.0).astype(bf16)
        chosen = jnp.dot(second_ref[...].astype(bf16), pick, preferred_element_type=f32)
        for kk in range(4):
            mine = lane128 // 32 == kk
            c = jnp.where(mine, chosen[:128], 0.0)
            s = jnp.where(mine, chosen[128:], 0.0)
            top, under = pl.ds(256 * kk, 128), pl.ds(256 * kk + 128, 128)
            re, im = slice(256 * late, 256 * late + 128), slice(256 * late + 128, 256 * late + 256)
            w2[top, re] = c.astype(bf16)
            w2[top, im] = (-s).astype(bf16)
            w2[under, re] = s.astype(bf16)
            w2[under, im] = c.astype(bf16)


def transform(dec, tw_ref, lhs2):
    def one(chunk, carry):
        values = [dec[pl.ds(PADROWS * j + 8 * chunk, 8), :] for j in range(SPLIT)]
        freq = real_fft(values)
        for k1 in range(32):
            ar, ai = freq[k1] if k1 <= 16 else freq[32 - k1]
            c = tw_ref[pl.ds(k1, 1), :]
            s = tw_ref[pl.ds(32 + k1, 1), :]
            if ai is None:
                br, bi = ar * c, ar * s
            elif k1 <= 16:
                br, bi = ar * c - ai * s, ar * s + ai * c
            else:
                br, bi = ar * c + ai * s, ar * s - ai * c
            rows = pl.ds((k1 // 4) * ROWS + 8 * chunk, 8)
            column = (k1 % 4) * 256
            lhs2[rows, column:column + 128] = br
            lhs2[rows, column + 128:column + 256] = bi
        return carry

    lax.fori_loop(0, 3, one, 0)


def whiten_slots(bands, live, y, wide):
    f32 = jnp.float32
    first, last, coarse, fine = band_edges(bands)
    slot = lax.broadcasted_iota(jnp.int32, (1, 128), 1)
    owner = slot % 32 // 8
    base = by_band(owner, coarse) + slot % 8
    offset = by_band(owner, fine)
    re, im, inside, counted = [], [], [], []
    for t in range(TILES):
        k1 = 4 * t + slot // 32
        late = k1 < offset
        bins = k1 + 32 * (base + jnp.where(late, 1, 0))
        rows = slice(ROWS * t, ROWS * t + ROWS)
        re.append(jnp.where(late, y[rows, 256:384], y[rows, 0:128]))
        im.append(jnp.where(late, y[rows, 384:512], y[rows, 128:256]))
        within = [(bins >= first[b]) & (bins < last[b]) for b in range(4)]
        inside.append(within)
        own = within[0] & (owner == 0)
        for b in range(1, 4):
            mine = within[b] & (owner == b)
            for earlier in range(b):
                mine = mine & jnp.logical_not(within[earlier])
            own = own | mine
        counted.append(own)
    station = lax.broadcasted_iota(jnp.int32, (ROWS, 1), 0)
    alive = jnp.where(station < 12, live[0].astype(f32), live[1].astype(f32))
    gains = [jnp.zeros((ROWS, 128), f32)] * TILES
    for b in range(4):
        total = jnp.zeros((ROWS, 128), f32)
        for t in range(TILES):
            power = re[t] * re[t] + im[t] * im[t]
            total = total + jnp.where(inside[t][b] & (owner == b), power, 0.0)
        width = (last[b] - first[b]).astype(f32)
        energy = jnp.sum(total, axis=1, keepdims=True) / width
        scale = lax.rsqrt(energy + 1e-06) * alive
        for t in range(TILES):
            gains[t] = gains[t] + jnp.where(inside[t][b], scale, 0.0)
    for t in range(TILES):
        gain = jnp.where(counted[t], gains[t], 0.0)
        wide[pl.ds(t, ROWS, stride=16), :] = re[t] * gain
        wide[pl.ds(8 + t, ROWS, stride=16), :] = im[t] * gain


def lag_groups(bands, quick_ref):
    f32 = jnp.float32
    _, _, coarse, fine = band_edges(bands)
    g = lax.broadcasted_iota(jnp.int32, (32, 128), 0)
    q = lax.broadcasted_iota(jnp.int32, (32, 128), 1)
    base = by_band(g // 8, coarse) + g % 8
    offset = by_band(g // 8, fine)
    tables = []
    for late in range(2):
        pick = jnp.where(q == base + late, 1.0, 0.0).astype(f32)
        quick = jnp.dot(pick, quick_ref[...], precision=HIGHEST, preferred_element_type=f32)
        quick = quick * f32(1.0 / math.sqrt(2048))
        tables.append((quick[:, :128], quick[:, 128:]))
    return base, offset, tables


def lag_tile(t, base, offset, tables, slow_ref, table):
    bf16 = jnp.bfloat16
    for kk in range(4):
        k1 = 4 * t + kk
        late = k1 < offset
        qc = jnp.where(late, tables[1][0], tables[0][0])
        qs = jnp.where(late, tables[1][1], tables[0][1])
        if k1 == 0:
            half = jnp.where(base + jnp.where(late, 1, 0) == 0, 0.5, 1.0)
            qc, qs = qc * half, qs * half
        row = 256 * t + 32 * kk
        for n in range(8):
            lanes = slice(128 * n, 128 * n + 128)
            sc = slow_ref[pl.ds(k1, 1), lanes]
            ss = slow_ref[pl.ds(32 + k1, 1), lanes]
            table[pl.ds(row, 32), lanes] = (sc * qc - ss * qs).astype(bf16)
            table[pl.ds(row + 128, 32), lanes] = (-(ss * qc + sc * qs)).astype(bf16)


def cross_block(left, got, cross, k, s):
    f32 = jnp.float32
    for i2 in range(2):
        for b in range(3):
            rre, rim = [], []
            for w in range(4):
                r = got[k * 8 + s, pl.ds((i2 * 12 + b * 4 + w) * 16, 16), :].astype(f32)
                rre.append(r[0:8])
                rim.append(r[8:16])
            for ia in range(6):
                re = im = None
                for w in range(4):
                    at = (ia * 4 + w) * 16
                    lre = left[at:at + 8, :]
                    lim = left[at + 8:at + 16, :]
                    pre = lre * rre[w] + lim * rim[w]
                    pim = lim * rre[w] - lre * rim[w]
                    re = pre if re is None else re + pre
                    im = pim if im is None else im + pim
                row = k * 288 + ia * 48 + s * 6 + i2 * 3 + b
                cross[pl.ds(row, 8, stride=1152), :] = re
                cross[pl.ds(row + 576, 8, stride=1152), :] = im


def whole_kernel(parts, bands_any, live_any, taps_any, kept_any, x_any, tw_any, second_any, slow_any, quick_any, out_ref,
                 bands, live, taps, kept, tw_ref, second_ref, slow_ref, quick_ref, in_sem, x_in, band_scr, lhs1, dec, lhs2, wide, w2, own_ref, got, cross, lhs, table,
                 x_sem, y_send, x_send, f_send, m_send, recv):
    f32, bf16 = jnp.float32, jnp.bfloat16
    section, grp, sta = lax.axis_index("section"), lax.axis_index("grp"), lax.axis_index("sta")
    groups = 16
    r = section * groups + grp
    mate = sta + 1 - 2 * lax.rem(sta, 2)
    right, across, left_peer = [lax.rem(sta + 2 * d, 8) for d in (1, 2, 3)]

    def group_at(shift):
        g = lax.rem(r + shift + 32, 32)
        return (g // groups, lax.rem(g, groups), sta)

    def near(s):
        return (section, grp, s)

    barrier = pltpu.get_barrier_semaphore()
    partners = [group_at(1), group_at(-1), near(mate), near(right), near(left_peer), near(across)]
    for who in partners:
        pl.semaphore_signal(barrier, inc=1, device_id=who, device_id_type=MESH)

    small = [
        pltpu.make_async_copy(source, place, in_sem.at[n])
        for n, (source, place) in enumerate([
            (taps_any, taps), (bands_any, bands), (second_any, second_ref), (tw_any, tw_ref), (live_any, live),
            (slow_any, slow_ref), (quick_any, quick_ref), (kept_any, kept),
        ])
    ]
    for copy in small:
        copy.start()
    fetches = [pltpu.make_async_copy(x_any.at[n], x_in.at[n], x_sem.at[n]) for n in range(6)]
    for fetch in fetches:
        fetch.start()
    for copy in small:
        copy.wait()
    weights = filter_weights(taps, band_scr)
    second_stage(bands, second_ref, w2)
    for fetch in fetches:
        fetch.wait()
    x = x_in[...].reshape(ROWS, -1)
    x = jnp.concatenate([x, jnp.zeros((PADROWS - ROWS, x.shape[1]), bf16)], axis=0)
    for j in range(SPLIT):
        rows = pl.ds(PADROWS * j, PADROWS)
        if j == 0:
            lhs1[rows, 0:128] = jnp.zeros((PADROWS, 128), bf16)
            lhs1[rows, 128:] = x[:, 0:512]
        else:
            lhs1[rows, :] = x[:, 512 * j - 128:512 * j + 512]
    summed = jnp.dot(lhs1[...], weights, preferred_element_type=f32)
    dec[...] = (summed[:, :128] + summed[:, 128:]).astype(bf16).astype(f32)
    transform(dec, tw_ref, lhs2)
    y = jnp.dot(lhs2[...].astype(bf16), w2[...], preferred_element_type=f32)
    whiten_slots(bands, live, y, wide)
    own_ref[...] = wide[...].astype(bf16)

    pl.semaphore_wait(barrier, len(partners))
    rows = own_ref.shape[0] // parts
    started = []

    def held(k, s, c):
        return got.at[k * 8 + s, pl.ds(c * rows, rows), :]

    def send(src, k, s, c, sem, who):
        copy = pltpu.make_async_remote_copy(
            src_ref=src, dst_ref=held(k, s, c), send_sem=sem, recv_sem=recv.at[k * 8 + s, c],
            device_id=who, device_id_type=MESH,
        )
        copy.start()
        started.append(copy)

    def arrived(k, s, c):
        pltpu.make_async_remote_copy(
            src_ref=held(k, s, c), dst_ref=held(k, s, c), send_sem=y_send.at[0, 0],
            recv_sem=recv.at[k * 8 + s, c], device_id=near(mate), device_id_type=MESH,
        ).wait_recv()

    def block(k, s):
        return got.at[k * 8 + s]

    def own_column(k, c):
        arrived(k, sta, c)
        if k == 0:
            send(held(0, sta, c), 0, sta, c, f_send.at[0, c], near(across))
            send(held(0, sta, c), 1, sta, c, y_send.at[1, c], group_at(1))
        send(held(k, sta, c), k, sta, c, x_send.at[k, 0, c], near(right))
        send(held(k, sta, c), k, sta, c, x_send.at[k, 1, c], near(left_peer))

    def far(k, c):
        arrived(k, across, c)
        if k == 0:
            send(held(0, across, c), 1, across, c, f_send.at[1, c], group_at(1))

    def to_mate(k, s, n):
        copy = pltpu.make_async_remote_copy(
            src_ref=block(k, s), dst_ref=block(k, s), send_sem=m_send.at[k, n], recv_sem=recv.at[k * 8 + s, 0],
            device_id=near(mate), device_id_type=MESH,
        )
        copy.start()
        started.append(copy)

    def side(k, s, n):
        for c in range(parts):
            arrived(k, s, c)
        to_mate(k, s, n)

    def by_mate(k, s):
        pltpu.make_async_remote_copy(
            src_ref=block(k, s), dst_ref=block(k, s), send_sem=m_send.at[k, 0], recv_sem=recv.at[k * 8 + s, 0],
            device_id=near(mate), device_id_type=MESH,
        ).wait_recv()

    def several(k, start, count):
        def one(n, carry):
            cross_block(wide, got, cross, k, lax.rem(start + 2 * n, 8))
            return carry
        lax.fori_loop(0, count, one, 0)

    def pack(k):
        rows = pl.ds(288 * k, 288)
        for t in range(TILES):
            for h in range(2):
                column = 256 * t + 128 * h
                lhs[rows, column:column + 128] = cross[pl.ds(1152 * t + 576 * h + 288 * k, 288), :].astype(bf16)

    def product(k, n):
        part = jnp.dot(lhs[pl.ds(288 * k, 288), :], table[:, 256 * n:256 * n + 256], preferred_element_type=f32)
        part = part * kept[k].astype(f32)
        for h in range(2):
            out_ref[pl.ds((2 * n + h) * 2 + k, 288, stride=16), :] = part[:, 128 * h:128 * h + 128]

    for c in range(parts):
        send(own_ref.at[pl.ds(c * rows, rows), :], 0, sta, c, y_send.at[0, c], group_at(1))
    base, offset, tables = lag_groups(bands, quick_ref)
    for t in range(3):
        lag_tile(t, base, offset, tables, slow_ref, table)
    for c in range(parts):
        own_column(0, c)
    to_mate(0, sta, 0)
    for t in range(3, 8):
        lag_tile(t, base, offset, tables, slow_ref, table)
    for c in range(parts):
        own_column(1, c)
    to_mate(1, sta, 0)
    several(0, sta, 1)
    for c in range(parts):
        far(0, c)
    to_mate(0, across, 3)
    side(0, left_peer, 1)
    side(0, right, 2)
    several(0, lax.rem(sta + 2, 8), 3)
    for d in range(4):
        by_mate(0, lax.rem(mate + 2 * d, 8))
    several(0, mate, 4)
    pack(0)
    for n in range(2):
        product(0, n)
    side(1, left_peer, 1)
    side(1, right, 2)
    for n in range(2, 4):
        product(0, n)
    for c in range(parts):
        far(1, c)
    to_mate(1, across, 3)
    several(1, sta, 4)
    for d in range(4):
        by_mate(1, lax.rem(mate + 2 * d, 8))
    several(1, mate, 4)
    pack(1)
    for n in range(4):
        product(1, n)
    for copy in started:
        copy.wait_send()


def vmem():
    return pl.BlockSpec(memory_space=pltpu.VMEM)


def body(records, fir_taps, band_bins, station_live, block_live):
    twiddle, second, slow, quick = constant_tables()
    f32, bf16 = jnp.float32, jnp.bfloat16
    x = jnp.transpose(records, (0, 2, 1, 3)).reshape(6, 4, -1)
    parts = 2
    dma = pltpu.SemaphoreType.DMA
    out = pl.pallas_call(
        functools.partial(whole_kernel, parts),
        out_shape=jax.ShapeDtypeStruct((288 * 16, 128), f32),
        in_specs=[pl.BlockSpec(memory_space=pltpu.HBM)] * 9,
        out_specs=vmem(),
        scratch_shapes=[
            pltpu.SMEM((2, 4), jnp.int32),
            pltpu.SMEM((2,), jnp.int32),
            pltpu.SMEM((64,), f32),
            pltpu.SMEM((2,), jnp.int32),
            pltpu.VMEM(twiddle.shape, f32),
            pltpu.VMEM(second.shape, f32),
            pltpu.VMEM(slow.shape, f32),
            pltpu.VMEM(quick.shape, f32),
            dma((8,)),
            pltpu.VMEM((6, 4, 16384), bf16),
            pltpu.VMEM((WINDOW, FRAMES), f32),
            pltpu.VMEM((PADROWS * SPLIT, WINDOW), bf16),
            pltpu.VMEM((PADROWS * SPLIT, FRAMES), f32),
            pltpu.VMEM((ROWS * TILES, 1024), f32),
            pltpu.VMEM((ROWS * 16, 128), f32),
            pltpu.VMEM((1024, 512), bf16),
            pltpu.VMEM((ROWS * 16, 128), bf16),
            pltpu.VMEM((16, ROWS * 16, 128), bf16),
            pltpu.VMEM((1152 * TILES, 128), f32),
            pltpu.VMEM((576, 2048), bf16),
            pltpu.VMEM((2048, 1024), bf16),
            dma((6,)),
            dma((2, parts)),
            dma((2, 2, parts)),
            dma((2, parts)),
            dma((2, 4)),
            dma((16, parts)),
        ],
        compiler_params=pltpu.CompilerParams(collective_id=0, has_side_effects=True, vmem_limit_bytes=VMEM_LIMIT),
        name="whole",
    )(*[
        pltpu.with_memory_space_constraint(operand, pltpu.HBM)
        for operand in (
            jnp.transpose(band_bins), station_live, fir_taps, block_live, x,
            jnp.asarray(twiddle), jnp.asarray(second), jnp.asarray(slow), jnp.asarray(quick),
        )
    ])
    out = out.reshape(288, 8, 2, 128)
    return jnp.transpose(out, (0, 2, 1, 3)).reshape(288, 2, 1024)


def solution(mesh):
    in_specs = (
        P(("section", "grp", "sta"), None, None, None),
        P(),
        P(),
        P(("section", "grp", "sta")),
        P(("section", "grp")),
    )
    out_specs = P("sta", ("section", "grp"), None)
    return jax.shard_map(body, mesh=mesh, in_specs=in_specs, out_specs=out_specs, check_vma=False)
```

```python
import functools
import math

import jax
import jax.numpy as jnp
import numpy as np
from jax import lax
from jax.experimental import pallas as pl
from jax.experimental.pallas import tpu as pltpu
from jax.sharding import PartitionSpec as P

ROWS = 24
PADROWS = 32
FRAMES = 128
SPLIT = 32
WINDOW = 640
TILES = 8
STEP = 1160
MESH = pl.DeviceIdType.MESH
VMEM_LIMIT = 40 * 1024 * 1024
HIGHEST = lax.Precision.HIGHEST


def constant_tables():
    i = np.arange(128)
    k = np.arange(32)[:, None]
    turn = 2.0 * np.pi / 4096
    twiddle = np.concatenate([np.cos(turn * k * i), -np.sin(turn * k * i)], 0).astype(np.float32)
    q = np.arange(64)
    fine = 2.0 * np.pi / 128 * (i[:, None] * q[None, :] % 128)
    second = np.concatenate([np.cos(fine), np.sin(fine)], 0).astype(np.float32)
    lag = np.arange(1024) - 512
    slow = turn * (k * lag[None, :] % 4096)
    lag_slow = np.concatenate([np.cos(slow), np.sin(slow)], 0).astype(np.float32)
    quick = np.zeros((128, 256))
    angle = 2.0 * np.pi / 128 * (q[:, None] * i[None, :] % 128)
    quick[:64, :128] = np.cos(angle)
    quick[:64, 128:] = np.sin(angle)
    return twiddle, second, lag_slow, quick.astype(np.float32)


def real_fft(values):
    n = len(values)
    if n == 2:
        return [(values[0] + values[1], None), (values[0] - values[1], None)]
    even = real_fft(values[0::2])
    odd = real_fft(values[1::2])
    result = [None] * (n // 2 + 1)
    for k in range(n // 4 + 1):
        er, ei = even[k]
        orr, oi = odd[k]
        c, s = math.cos(2 * math.pi * k / n), math.sin(2 * math.pi * k / n)
        if k == 0:
            tr, ti = orr, oi
        elif 4 * k == n:
            tr, ti = oi, -orr
        elif oi is None:
            tr, ti = orr * c, orr * (-s)
        else:
            tr, ti = orr * c + oi * s, oi * c - orr * s
        def plus(a, b):
            return b if a is None else a if b is None else a + b
        def minus(a, b):
            return (None if b is None else -b) if a is None else a if b is None else a - b
        result[k] = (plus(er, tr), plus(ei, ti))
        if n // 2 - k != k:
            low = minus(ti, ei)
            result[n // 2 - k] = (minus(er, tr), low)
    return result


def filter_weights(taps, band_scr):
    f32, bf16 = jnp.float32, jnp.bfloat16
    a_index = lax.broadcasted_iota(jnp.int32, (WINDOW // 4, FRAMES), 0)
    o_index = lax.broadcasted_iota(jnp.int32, (WINDOW // 4, FRAMES), 1)
    lead = o_index - a_index + 32
    pieces = [jnp.zeros((WINDOW // 4, FRAMES), f32)] * 4
    for d in range(17):
        here = lead == d
        for b in range(4):
            if 0 <= 4 * d - b < 64:
                pieces[b] = jnp.where(here, taps[4 * d - b], pieces[b])
    for b in range(4):
        band_scr[pl.ds(b, WINDOW // 4, stride=4), :] = pieces[b]
    band = band_scr[...]
    high = band.astype(bf16)
    low = (band - high.astype(f32)).astype(bf16)
    return jnp.concatenate([high, low], axis=1)


def by_band(index, values):
    result = jnp.full(index.shape, values[3], jnp.int32)
    for b in range(3):
        result = jnp.where(index == b, values[b], result)
    return result


def band_edges(bands):
    first = [bands[0, b] for b in range(4)]
    last = [bands[1, b] for b in range(4)]
    return first, last, [s // 32 for s in first], [s % 32 for s in first]


def second_stage(bands, second_ref, w2):
    f32, bf16 = jnp.float32, jnp.bfloat16
    _, _, coarse, _ = band_edges(bands)
    q = lax.broadcasted_iota(jnp.int32, (64, 128), 0)
    lane = lax.broadcasted_iota(jnp.int32, (64, 128), 1)
    base = by_band(lane % 32 // 8, coarse) + lane % 8
    lane128 = lax.broadcasted_iota(jnp.int32, (128, 128), 1)
    for late in range(2):
        pick = jnp.where(q == base + late, 1.0, 0.0).astype(bf16)
        chosen = jnp.dot(second_ref[...].astype(bf16), pick, preferred_element_type=f32)
        for kk in range(4):
            mine = lane128 // 32 == kk
            c = jnp.where(mine, chosen[:128], 0.0)
            s = jnp.where(mine, chosen[128:], 0.0)
            top, under = pl.ds(256 * kk, 128), pl.ds(256 * kk + 128, 128)
            re, im = slice(256 * late, 256 * late + 128), slice(256 * late + 128, 256 * late + 256)
            w2[top, re] = c.astype(bf16)
            w2[top, im] = (-s).astype(bf16)
            w2[under, re] = s.astype(bf16)
            w2[under, im] = c.astype(bf16)


def transform(dec, tw_ref, lhs2):
    def one(chunk, carry):
        values = [dec[pl.ds(PADROWS * j + 8 * chunk, 8), :] for j in range(SPLIT)]
        freq = real_fft(values)
        for k1 in range(32):
            ar, ai = freq[k1] if k1 <= 16 else freq[32 - k1]
            c = tw_ref[pl.ds(k1, 1), :]
            s = tw_ref[pl.ds(32 + k1, 1), :]
            if ai is None:
                br, bi = ar * c, ar * s
            elif k1 <= 16:
                br, bi = ar * c - ai * s, ar * s + ai * c
            else:
                br, bi = ar * c + ai * s, ar * s - ai * c
            rows = pl.ds((k1 // 4) * ROWS + 8 * chunk, 8)
            column = (k1 % 4) * 256
            lhs2[rows, column:column + 128] = br
            lhs2[rows, column + 128:column + 256] = bi
        return carry

    lax.fori_loop(0, 3, one, 0)


def whiten_slots(bands, live, y, wide):
    f32 = jnp.float32
    first, last, coarse, fine = band_edges(bands)
    slot = lax.broadcasted_iota(jnp.int32, (1, 128), 1)
    owner = slot % 32 // 8
    base = by_band(owner, coarse) + slot % 8
    offset = by_band(owner, fine)
    re, im, inside, counted = [], [], [], []
    for t in range(TILES):
        k1 = 4 * t + slot // 32
        late = k1 < offset
        bins = k1 + 32 * (base + jnp.where(late, 1, 0))
        rows = slice(ROWS * t, ROWS * t + ROWS)
        re.append(jnp.where(late, y[rows, 256:384], y[rows, 0:128]))
        im.append(jnp.where(late, y[rows, 384:512], y[rows, 128:256]))
        within = [(bins >= first[b]) & (bins < last[b]) for b in range(4)]
        inside.append(within)
        own = within[0] & (owner == 0)
        for b in range(1, 4):
            mine = within[b] & (owner == b)
            for earlier in range(b):
                mine = mine & jnp.logical_not(within[earlier])
            own = own | mine
        counted.append(own)
    station = lax.broadcasted_iota(jnp.int32, (ROWS, 1), 0)
    alive = jnp.where(station < 12, live[0].astype(f32), live[1].astype(f32))
    gains = [jnp.zeros((ROWS, 128), f32)] * TILES
    for b in range(4):
        total = jnp.zeros((ROWS, 128), f32)
        for t in range(TILES):
            power = re[t] * re[t] + im[t] * im[t]
            total = total + jnp.where(inside[t][b] & (owner == b), power, 0.0)
        width = (last[b] - first[b]).astype(f32)
        energy = jnp.sum(total, axis=1, keepdims=True) / width
        scale = lax.rsqrt(energy + 1e-06) * alive
        for t in range(TILES):
            gains[t] = gains[t] + jnp.where(inside[t][b], scale, 0.0)
    for t in range(TILES):
        gain = jnp.where(counted[t], gains[t], 0.0)
        wide[pl.ds(t, ROWS, stride=16), :] = re[t] * gain
        wide[pl.ds(8 + t, ROWS, stride=16), :] = im[t] * gain


def lag_groups(bands, quick_ref):
    f32 = jnp.float32
    _, _, coarse, fine = band_edges(bands)
    g = lax.broadcasted_iota(jnp.int32, (32, 128), 0)
    q = lax.broadcasted_iota(jnp.int32, (32, 128), 1)
    base = by_band(g // 8, coarse) + g % 8
    offset = by_band(g // 8, fine)
    tables = []
    for late in range(2):
        pick = jnp.where(q == base + late, 1.0, 0.0).astype(f32)
        quick = jnp.dot(pick, quick_ref[...], precision=HIGHEST, preferred_element_type=f32)
        quick = quick * f32(1.0 / math.sqrt(2048))
        tables.append((quick[:, :128], quick[:, 128:]))
    return base, offset, tables


def lag_tile(t, base, offset, tables, slow_ref, table):
    bf16 = jnp.bfloat16
    for kk in range(4):
        k1 = 4 * t + kk
        late = k1 < offset
        qc = jnp.where(late, tables[1][0], tables[0][0])
        qs = jnp.where(late, tables[1][1], tables[0][1])
        if k1 == 0:
            half = jnp.where(base + jnp.where(late, 1, 0) == 0, 0.5, 1.0)
            qc, qs = qc * half, qs * half
        row = 256 * t + 32 * kk
        for n in range(8):
            lanes = slice(128 * n, 128 * n + 128)
            sc = slow_ref[pl.ds(k1, 1), lanes]
            ss = slow_ref[pl.ds(32 + k1, 1), lanes]
            table[pl.ds(row, 32), lanes] = (sc * qc - ss * qs).astype(bf16)
            table[pl.ds(row + 128, 32), lanes] = (-(ss * qc + sc * qs)).astype(bf16)


def cross_block(left, got, cross, k, s):
    f32 = jnp.float32
    for i2 in range(2):
        for b in range(3):
            rre, rim = [], []
            for w in range(4):
                r = got[k * 8 + s, pl.ds((i2 * 12 + b * 4 + w) * 16, 16), :].astype(f32)
                rre.append(r[0:8])
                rim.append(r[8:16])
            for ia in range(6):
                re = im = None
                for w in range(4):
                    at = (ia * 4 + w) * 16
                    lre = left[at:at + 8, :]
                    lim = left[at + 8:at + 16, :]
                    pre = lre * rre[w] + lim * rim[w]
                    pim = lim * rre[w] - lre * rim[w]
                    re = pre if re is None else re + pre
                    im = pim if im is None else im + pim
                row = k * 288 + ia * 48 + s * 6 + i2 * 3 + b
                cross[pl.ds(row, 8, stride=STEP), :] = re
                cross[pl.ds(row + 576, 8, stride=STEP), :] = im


def whole_kernel(parts, bands_any, live_any, taps_any, kept_any, x_any, tw_any, second_any, slow_any, quick_any, out_ref,
                 bands, live, taps, kept, tw_ref, second_ref, slow_ref, quick_ref, in_sem, x_in, band_scr, lhs1, dec, lhs2, wide, w2, own_ref, got, cross, lhs, table,
                 x_sem, y_send, x_send, f_send, m_send, recv):
    f32, bf16 = jnp.float32, jnp.bfloat16
    section, grp, sta = lax.axis_index("section"), lax.axis_index("grp"), lax.axis_index("sta")
    groups = 16
    r = section * groups + grp
    mate = sta + 1 - 2 * lax.rem(sta, 2)
    right, across, left_peer = [lax.rem(sta + 2 * d, 8) for d in (1, 2, 3)]

    def group_at(shift):
        g = lax.rem(r + shift + 32, 32)
        return (g // groups, lax.rem(g, groups), sta)

    def near(s):
        return (section, grp, s)

    barrier = pltpu.get_barrier_semaphore()
    partners = [group_at(1), group_at(-1), near(mate), near(right), near(left_peer), near(across)]
    for who in partners:
        pl.semaphore_signal(barrier, inc=1, device_id=who, device_id_type=MESH)

    small = [
        pltpu.make_async_copy(source, place, in_sem.at[n])
        for n, (source, place) in enumerate([
            (taps_any, taps), (bands_any, bands), (second_any, second_ref), (tw_any, tw_ref), (live_any, live),
            (quick_any, quick_ref), (slow_any, slow_ref), (kept_any, kept),
        ])
    ]
    for copy in small[:3]:
        copy.start()
    fetches = [pltpu.make_async_copy(x_any.at[n], x_in.at[n], x_sem.at[n]) for n in range(6)]
    for fetch in fetches:
        fetch.start()
    for copy in small[3:]:
        copy.start()
    small[0].wait()
    weights = filter_weights(taps, band_scr)
    small[1].wait()
    small[2].wait()
    second_stage(bands, second_ref, w2)
    for fetch in fetches:
        fetch.wait()
    x = x_in[...].reshape(ROWS, -1)
    x = jnp.concatenate([x, jnp.zeros((PADROWS - ROWS, x.shape[1]), bf16)], axis=0)
    for j in range(SPLIT):
        rows = pl.ds(PADROWS * j, PADROWS)
        if j == 0:
            lhs1[rows, 0:128] = jnp.zeros((PADROWS, 128), bf16)
            lhs1[rows, 128:] = x[:, 0:512]
        else:
            lhs1[rows, :] = x[:, 512 * j - 128:512 * j + 512]
    summed = jnp.dot(lhs1[...], weights, preferred_element_type=f32)
    dec[...] = (summed[:, :128] + summed[:, 128:]).astype(bf16).astype(f32)
    small[3].wait()
    small[4].wait()
    transform(dec, tw_ref, lhs2)
    y = jnp.dot(lhs2[...].astype(bf16), w2[...], preferred_element_type=f32)
    whiten_slots(bands, live, y, wide)
    own_ref[...] = wide[...].astype(bf16)

    pl.semaphore_wait(barrier, len(partners))
    rows = own_ref.shape[0] // parts
    started = []

    def held(k, s, c):
        return got.at[k * 8 + s, pl.ds(c * rows, rows), :]

    def send(src, k, s, c, sem, who):
        copy = pltpu.make_async_remote_copy(
            src_ref=src, dst_ref=held(k, s, c), send_sem=sem, recv_sem=recv.at[k * 8 + s, c],
            device_id=who, device_id_type=MESH,
        )
        copy.start()
        started.append(copy)

    def arrived(k, s, c):
        pltpu.make_async_remote_copy(
            src_ref=held(k, s, c), dst_ref=held(k, s, c), send_sem=y_send.at[0, 0],
            recv_sem=recv.at[k * 8 + s, c], device_id=near(mate), device_id_type=MESH,
        ).wait_recv()

    def block(k, s):
        return got.at[k * 8 + s]

    def own_column(k, c):
        arrived(k, sta, c)
        if k == 0:
            send(held(0, sta, c), 0, sta, c, f_send.at[0, c], near(across))
            send(held(0, sta, c), 1, sta, c, y_send.at[1, c], group_at(1))
        send(held(k, sta, c), k, sta, c, x_send.at[k, 0, c], near(right))
        send(held(k, sta, c), k, sta, c, x_send.at[k, 1, c], near(left_peer))

    def far(k, c):
        arrived(k, across, c)
        if k == 0:
            send(held(0, across, c), 1, across, c, f_send.at[1, c], group_at(1))

    def to_mate(k, s, n):
        copy = pltpu.make_async_remote_copy(
            src_ref=block(k, s), dst_ref=block(k, s), send_sem=m_send.at[k, n], recv_sem=recv.at[k * 8 + s, 0],
            device_id=near(mate), device_id_type=MESH,
        )
        copy.start()
        started.append(copy)

    def side(k, s, n):
        for c in range(parts):
            arrived(k, s, c)
        to_mate(k, s, n)

    def by_mate(k, s):
        pltpu.make_async_remote_copy(
            src_ref=block(k, s), dst_ref=block(k, s), send_sem=m_send.at[k, 0], recv_sem=recv.at[k * 8 + s, 0],
            device_id=near(mate), device_id_type=MESH,
        ).wait_recv()

    def several(k, start, count, waiting=False):
        def one(n, carry):
            s = lax.rem(start + 2 * n, 8)
            if waiting:
                by_mate(k, s)
            cross_block(wide, got, cross, k, s)
            return carry
        lax.fori_loop(0, count, one, 0)

    def pack(k):
        rows = pl.ds(288 * k, 288)
        for t in range(TILES):
            for h in range(2):
                column = 256 * t + 128 * h
                lhs[rows, column:column + 128] = cross[pl.ds(STEP * t + 576 * h + 288 * k, 288), :].astype(bf16)

    def product(k, n):
        part = jnp.dot(lhs[pl.ds(288 * k, 288), :], table[:, 256 * n:256 * n + 256], preferred_element_type=f32)
        part = part * kept[k].astype(f32)
        for h in range(2):
            out_ref[pl.ds((2 * n + h) * 2 + k, 288, stride=16), :] = part[:, 128 * h:128 * h + 128]

    for c in range(parts):
        send(own_ref.at[pl.ds(c * rows, rows), :], 0, sta, c, y_send.at[0, c], group_at(1))
    for copy in small[5:]:
        copy.wait()
    base, offset, tables = lag_groups(bands, quick_ref)
    for t in range(3):
        lag_tile(t, base, offset, tables, slow_ref, table)
    for c in range(parts):
        own_column(0, c)
    to_mate(0, sta, 0)
    for t in range(3, 8):
        lag_tile(t, base, offset, tables, slow_ref, table)
    for c in range(parts):
        own_column(1, c)
    to_mate(1, sta, 0)
    several(0, sta, 1)
    for c in range(parts):
        far(0, c)
    to_mate(0, across, 3)
    side(0, left_peer, 1)
    side(0, right, 2)
    several(0, lax.rem(sta + 2, 8), 3)
    for d in range(4):
        by_mate(0, lax.rem(mate + 2 * d, 8))
    several(0, mate, 4)
    pack(0)
    for n in range(0, 4):
        product(0, n)
    side(1, left_peer, 1)
    side(1, right, 2)
    for c in range(parts):
        far(1, c)
    to_mate(1, across, 3)
    several(1, sta, 4)
    several(1, lax.rem(mate + 6, 8), 3, True)
    for copy in started:
        copy.wait_send()
    several(1, lax.rem(mate + 4, 8), 1, True)
    pack(1)
    for n in range(4):
        product(1, n)


def vmem():
    return pl.BlockSpec(memory_space=pltpu.VMEM)


def body(records, fir_taps, band_bins, station_live, block_live):
    twiddle, second, slow, quick = constant_tables()
    f32, bf16 = jnp.float32, jnp.bfloat16
    x = jnp.transpose(records, (0, 2, 1, 3)).reshape(6, 4, -1)
    parts = 2
    dma = pltpu.SemaphoreType.DMA
    out = pl.pallas_call(
        functools.partial(whole_kernel, parts),
        out_shape=jax.ShapeDtypeStruct((288 * 16, 128), f32),
        in_specs=[pl.BlockSpec(memory_space=pltpu.HBM)] * 9,
        out_specs=vmem(),
        scratch_shapes=[
            pltpu.SMEM((2, 4), jnp.int32),
            pltpu.SMEM((2,), jnp.int32),
            pltpu.SMEM((64,), f32),
            pltpu.SMEM((2,), jnp.int32),
            pltpu.VMEM(twiddle.shape, f32),
            pltpu.VMEM(second.shape, f32),
            pltpu.VMEM(slow.shape, f32),
            pltpu.VMEM(quick.shape, f32),
            dma((8,)),
            pltpu.VMEM((6, 4, 16384), bf16),
            pltpu.VMEM((WINDOW, FRAMES), f32),
            pltpu.VMEM((PADROWS * SPLIT, WINDOW), bf16),
            pltpu.VMEM((PADROWS * SPLIT, FRAMES), f32),
            pltpu.VMEM((ROWS * TILES, 1024), f32),
            pltpu.VMEM((ROWS * 16, 128), f32),
            pltpu.VMEM((1024, 512), bf16),
            pltpu.VMEM((ROWS * 16, 128), bf16),
            pltpu.VMEM((16, ROWS * 16, 128), bf16),
            pltpu.VMEM((STEP * TILES, 128), f32),
            pltpu.VMEM((576, 2048), bf16),
            pltpu.VMEM((2048, 1024), bf16),
            dma((6,)),
            dma((2, parts)),
            dma((2, 2, parts)),
            dma((2, parts)),
            dma((2, 4)),
            dma((16, parts)),
        ],
        compiler_params=pltpu.CompilerParams(collective_id=0, has_side_effects=True, vmem_limit_bytes=VMEM_LIMIT),
        name="whole",
    )(*[
        pltpu.with_memory_space_constraint(operand, pltpu.HBM)
        for operand in (
            jnp.transpose(band_bins), station_live, fir_taps, block_live, x,
            jnp.asarray(twiddle), jnp.asarray(second), jnp.asarray(slow), jnp.asarray(quick),
        )
    ])
    out = out.reshape(288, 8, 2, 128)
    return jnp.transpose(out, (0, 2, 1, 3)).reshape(288, 2, 1024)


def solution(mesh):
    in_specs = (
        P(("section", "grp", "sta"), None, None, None),
        P(),
        P(),
        P(("section", "grp", "sta")),
        P(("section", "grp")),
    )
    out_specs = P("sta", ("section", "grp"), None)
    return jax.shard_map(body, mesh=mesh, in_specs=in_specs, out_specs=out_specs, check_vma=False)
```

```python
import functools
import math

import jax
import jax.numpy as jnp
import numpy as np
from jax import lax
from jax.experimental import pallas as pl
from jax.experimental.pallas import tpu as pltpu
from jax.sharding import PartitionSpec as P

ROWS = 24
FRAMES = 128
SPLIT = 32
WINDOW = 640
TILES = 8
STEP = 1160
MESH = pl.DeviceIdType.MESH
VMEM_LIMIT = 40 * 1024 * 1024
HIGHEST = lax.Precision.HIGHEST


def constant_tables():
    i = np.arange(128)
    k = np.arange(32)[:, None]
    turn = 2.0 * np.pi / 4096
    twiddle = np.concatenate([np.cos(turn * k * i), -np.sin(turn * k * i)], 0).astype(np.float32)
    q = np.arange(64)
    fine = 2.0 * np.pi / 128 * (i[:, None] * q[None, :] % 128)
    second = np.concatenate([np.cos(fine), np.sin(fine)], 0).astype(np.float32)
    lag = np.arange(1024) - 512
    slow = turn * (k * lag[None, :] % 4096)
    lag_slow = np.concatenate([np.cos(slow), np.sin(slow)], 0).astype(np.float32)
    quick = np.zeros((128, 256))
    angle = 2.0 * np.pi / 128 * (q[:, None] * i[None, :] % 128)
    quick[:64, :128] = np.cos(angle)
    quick[:64, 128:] = np.sin(angle)
    return twiddle, second, lag_slow, quick.astype(np.float32)


def real_fft(values):
    n = len(values)
    if n == 2:
        return [(values[0] + values[1], None), (values[0] - values[1], None)]
    even = real_fft(values[0::2])
    odd = real_fft(values[1::2])
    result = [None] * (n // 2 + 1)
    for k in range(n // 4 + 1):
        er, ei = even[k]
        orr, oi = odd[k]
        c, s = math.cos(2 * math.pi * k / n), math.sin(2 * math.pi * k / n)
        if k == 0:
            tr, ti = orr, oi
        elif 4 * k == n:
            tr, ti = oi, -orr
        elif oi is None:
            tr, ti = orr * c, orr * (-s)
        else:
            tr, ti = orr * c + oi * s, oi * c - orr * s
        def plus(a, b):
            return b if a is None else a if b is None else a + b
        def minus(a, b):
            return (None if b is None else -b) if a is None else a if b is None else a - b
        result[k] = (plus(er, tr), plus(ei, ti))
        if n // 2 - k != k:
            low = minus(ti, ei)
            result[n // 2 - k] = (minus(er, tr), low)
    return result


def filter_weights(taps, band_scr):
    f32, bf16 = jnp.float32, jnp.bfloat16
    a_index = lax.broadcasted_iota(jnp.int32, (WINDOW // 4, FRAMES), 0)
    o_index = lax.broadcasted_iota(jnp.int32, (WINDOW // 4, FRAMES), 1)
    lead = o_index - a_index + 32
    pieces = [jnp.zeros((WINDOW // 4, FRAMES), f32)] * 4
    for d in range(17):
        here = lead == d
        for b in range(4):
            if 0 <= 4 * d - b < 64:
                pieces[b] = jnp.where(here, taps[4 * d - b], pieces[b])
    for b in range(4):
        band_scr[pl.ds(b, WINDOW // 4, stride=4), :] = pieces[b]
    band = band_scr[...]
    high = band.astype(bf16)
    low = (band - high.astype(f32)).astype(bf16)
    return jnp.concatenate([high, low], axis=1)


def by_band(index, values):
    result = jnp.full(index.shape, values[3], jnp.int32)
    for b in range(3):
        result = jnp.where(index == b, values[b], result)
    return result


def band_edges(bands):
    first = [bands[0, b] for b in range(4)]
    last = [bands[1, b] for b in range(4)]
    return first, last, [s // 32 for s in first], [s % 32 for s in first]


def second_stage(bands, second_ref, w2):
    f32, bf16 = jnp.float32, jnp.bfloat16
    _, _, coarse, _ = band_edges(bands)
    q = lax.broadcasted_iota(jnp.int32, (64, 128), 0)
    lane = lax.broadcasted_iota(jnp.int32, (64, 128), 1)
    base = by_band(lane % 32 // 8, coarse) + lane % 8
    lane128 = lax.broadcasted_iota(jnp.int32, (128, 128), 1)
    for late in range(2):
        pick = jnp.where(q == base + late, 1.0, 0.0).astype(bf16)
        chosen = jnp.dot(second_ref[...].astype(bf16), pick, preferred_element_type=f32)
        for kk in range(4):
            mine = lane128 // 32 == kk
            c = jnp.where(mine, chosen[:128], 0.0)
            s = jnp.where(mine, chosen[128:], 0.0)
            top, under = pl.ds(256 * kk, 128), pl.ds(256 * kk + 128, 128)
            re, im = slice(256 * late, 256 * late + 128), slice(256 * late + 128, 256 * late + 256)
            w2[top, re] = c.astype(bf16)
            w2[top, im] = (-s).astype(bf16)
            w2[under, re] = s.astype(bf16)
            w2[under, im] = c.astype(bf16)


def transform(chunk, dec, tw_ref, lhs2):
    values = [dec[pl.ds(256 * chunk + 8 * j, 8), :] for j in range(SPLIT)]
    freq = real_fft(values)
    for k1 in range(32):
        ar, ai = freq[k1] if k1 <= 16 else freq[32 - k1]
        c = tw_ref[pl.ds(k1, 1), :]
        s = tw_ref[pl.ds(32 + k1, 1), :]
        if ai is None:
            br, bi = ar * c, ar * s
        elif k1 <= 16:
            br, bi = ar * c - ai * s, ar * s + ai * c
        else:
            br, bi = ar * c + ai * s, ar * s - ai * c
        rows = pl.ds((k1 // 4) * ROWS + 8 * chunk, 8)
        column = (k1 % 4) * 256
        lhs2[rows, column:column + 128] = br
        lhs2[rows, column + 128:column + 256] = bi


def whiten_slots(bands, live, y, wide):
    f32 = jnp.float32
    first, last, coarse, fine = band_edges(bands)
    slot = lax.broadcasted_iota(jnp.int32, (1, 128), 1)
    owner = slot % 32 // 8
    base = by_band(owner, coarse) + slot % 8
    offset = by_band(owner, fine)
    re, im, inside, counted = [], [], [], []
    for t in range(TILES):
        k1 = 4 * t + slot // 32
        late = k1 < offset
        bins = k1 + 32 * (base + jnp.where(late, 1, 0))
        rows = slice(ROWS * t, ROWS * t + ROWS)
        re.append(jnp.where(late, y[rows, 256:384], y[rows, 0:128]))
        im.append(jnp.where(late, y[rows, 384:512], y[rows, 128:256]))
        within = [(bins >= first[b]) & (bins < last[b]) for b in range(4)]
        inside.append(within)
        own = within[0] & (owner == 0)
        for b in range(1, 4):
            mine = within[b] & (owner == b)
            for earlier in range(b):
                mine = mine & jnp.logical_not(within[earlier])
            own = own | mine
        counted.append(own)
    station = lax.broadcasted_iota(jnp.int32, (ROWS, 1), 0)
    alive = jnp.where(station < 12, live[0].astype(f32), live[1].astype(f32))
    gains = [jnp.zeros((ROWS, 128), f32)] * TILES
    for b in range(4):
        total = jnp.zeros((ROWS, 128), f32)
        for t in range(TILES):
            power = re[t] * re[t] + im[t] * im[t]
            total = total + jnp.where(inside[t][b] & (owner == b), power, 0.0)
        width = (last[b] - first[b]).astype(f32)
        energy = jnp.sum(total, axis=1, keepdims=True) / width
        scale = lax.rsqrt(energy + 1e-06) * alive
        for t in range(TILES):
            gains[t] = gains[t] + jnp.where(inside[t][b], scale, 0.0)
    for t in range(TILES):
        gain = jnp.where(counted[t], gains[t], 0.0)
        wide[pl.ds(t, ROWS, stride=16), :] = re[t] * gain
        wide[pl.ds(8 + t, ROWS, stride=16), :] = im[t] * gain


def lag_groups(bands, quick_ref):
    f32 = jnp.float32
    _, _, coarse, fine = band_edges(bands)
    g = lax.broadcasted_iota(jnp.int32, (32, 128), 0)
    q = lax.broadcasted_iota(jnp.int32, (32, 128), 1)
    base = by_band(g // 8, coarse) + g % 8
    offset = by_band(g // 8, fine)
    tables = []
    for late in range(2):
        pick = jnp.where(q == base + late, 1.0, 0.0).astype(f32)
        quick = jnp.dot(pick, quick_ref[...], precision=HIGHEST, preferred_element_type=f32)
        quick = quick * f32(1.0 / math.sqrt(2048))
        tables.append((quick[:, :128], quick[:, 128:]))
    return base, offset, tables


def lag_tile(t, base, offset, tables, slow_ref, table):
    bf16 = jnp.bfloat16
    for kk in range(4):
        k1 = 4 * t + kk
        late = k1 < offset
        qc = jnp.where(late, tables[1][0], tables[0][0])
        qs = jnp.where(late, tables[1][1], tables[0][1])
        if k1 == 0:
            half = jnp.where(base + jnp.where(late, 1, 0) == 0, 0.5, 1.0)
            qc, qs = qc * half, qs * half
        row = 256 * t + 32 * kk
        for n in range(8):
            lanes = slice(128 * n, 128 * n + 128)
            sc = slow_ref[pl.ds(k1, 1), lanes]
            ss = slow_ref[pl.ds(32 + k1, 1), lanes]
            table[pl.ds(row, 32), lanes] = (sc * qc - ss * qs).astype(bf16)
            table[pl.ds(row + 128, 32), lanes] = (-(ss * qc + sc * qs)).astype(bf16)


def cross_block(left, got, cross, k, s):
    f32 = jnp.float32
    for i2 in range(2):
        for b in range(3):
            rre, rim = [], []
            for w in range(4):
                r = got[k * 8 + s, pl.ds((i2 * 12 + b * 4 + w) * 16, 16), :].astype(f32)
                rre.append(r[0:8])
                rim.append(r[8:16])
            for ia in range(6):
                re = im = None
                for w in range(4):
                    at = (ia * 4 + w) * 16
                    lre = left[at:at + 8, :]
                    lim = left[at + 8:at + 16, :]
                    pre = lre * rre[w] + lim * rim[w]
                    pim = lim * rre[w] - lre * rim[w]
                    re = pre if re is None else re + pre
                    im = pim if im is None else im + pim
                row = k * 288 + ia * 48 + s * 6 + i2 * 3 + b
                cross[pl.ds(row, 8, stride=STEP), :] = re
                cross[pl.ds(row + 576, 8, stride=STEP), :] = im


def whole_kernel(parts, bands_any, live_any, taps_any, kept_any, x_any, tw_any, second_any, slow_any, quick_any, out_ref,
                 bands, live, taps, kept, tw_ref, second_ref, slow_ref, quick_ref, in_sem, x_in, band_scr, lhs1, dec, lhs2, wide, w2, own_ref, got, cross, lhs, table,
                 x_sem, y_send, x_send, f_send, m_send, recv):
    f32, bf16 = jnp.float32, jnp.bfloat16
    section, grp, sta = lax.axis_index("section"), lax.axis_index("grp"), lax.axis_index("sta")
    groups = 16
    r = section * groups + grp
    mate = sta + 1 - 2 * lax.rem(sta, 2)
    right, across, left_peer = [lax.rem(sta + 2 * d, 8) for d in (1, 2, 3)]

    def group_at(shift):
        g = lax.rem(r + shift + 32, 32)
        return (g // groups, lax.rem(g, groups), sta)

    def near(s):
        return (section, grp, s)

    barrier = pltpu.get_barrier_semaphore()
    partners = [group_at(1), group_at(-1), near(mate), near(right), near(left_peer), near(across)]
    for who in partners:
        pl.semaphore_signal(barrier, inc=1, device_id=who, device_id_type=MESH)

    small = [
        pltpu.make_async_copy(source, place, in_sem.at[n])
        for n, (source, place) in enumerate([
            (taps_any, taps), (bands_any, bands), (second_any, second_ref), (tw_any, tw_ref), (live_any, live),
            (quick_any, quick_ref), (slow_any, slow_ref), (kept_any, kept),
        ])
    ]
    for copy in small[:3]:
        copy.start()
    fetches = [pltpu.make_async_copy(x_any.at[n], x_in.at[n], x_sem.at[n]) for n in range(6)]
    for fetch in fetches:
        fetch.start()
    for copy in small[3:]:
        copy.start()
    small[0].wait()
    weights = filter_weights(taps, band_scr)
    small[1].wait()
    small[2].wait()
    second_stage(bands, second_ref, w2)
    small[3].wait()
    small[4].wait()
    for chunk in range(3):
        fetches[2 * chunk].wait()
        fetches[2 * chunk + 1].wait()
        x = x_in[2 * chunk:2 * chunk + 2].reshape(8, -1)
        edge = jnp.concatenate([jnp.zeros((8, 128), bf16), x[:, 0:512]], axis=1)
        first = 256 * chunk
        for j in range(0, SPLIT, 2):
            head = edge if j == 0 else x[:, 512 * j - 128:512 * j + 512]
            both = jnp.concatenate([head, x[:, 512 * j + 384:512 * j + 1024]], axis=0)
            lhs1[pl.ds(first + 8 * j, 16), :] = both
        summed = jnp.dot(lhs1[pl.ds(first, 256), :], weights, preferred_element_type=f32)
        dec[pl.ds(first, 256), :] = (summed[:, :128] + summed[:, 128:]).astype(bf16).astype(f32)
        transform(chunk, dec, tw_ref, lhs2)
    y = jnp.dot(lhs2[...].astype(bf16), w2[...], preferred_element_type=f32)
    whiten_slots(bands, live, y, wide)
    own_ref[...] = wide[...].astype(bf16)

    pl.semaphore_wait(barrier, len(partners))
    rows = own_ref.shape[0] // parts
    started = []

    def held(k, s, c):
        return got.at[k * 8 + s, pl.ds(c * rows, rows), :]

    def send(src, k, s, c, sem, who):
        copy = pltpu.make_async_remote_copy(
            src_ref=src, dst_ref=held(k, s, c), send_sem=sem, recv_sem=recv.at[k * 8 + s, c],
            device_id=who, device_id_type=MESH,
        )
        copy.start()
        started.append(copy)

    def arrived(k, s, c):
        pltpu.make_async_remote_copy(
            src_ref=held(k, s, c), dst_ref=held(k, s, c), send_sem=y_send.at[0, 0],
            recv_sem=recv.at[k * 8 + s, c], device_id=near(mate), device_id_type=MESH,
        ).wait_recv()

    def block(k, s):
        return got.at[k * 8 + s]

    def own_column(k, c):
        arrived(k, sta, c)
        if k == 0:
            send(held(0, sta, c), 0, sta, c, f_send.at[0, c], near(across))
            send(held(0, sta, c), 1, sta, c, y_send.at[1, c], group_at(1))
            send(held(k, sta, c), k, sta, c, x_send.at[k, 0, c], near(right))
            send(held(k, sta, c), k, sta, c, x_send.at[k, 1, c], near(left_peer))
        elif c == parts - 1:
            to_peer(1, sta, x_send.at[1, 0, 0], near(right))
            to_peer(1, sta, x_send.at[1, 1, 0], near(left_peer))

    def far(k, c):
        arrived(k, across, c)
        if k == 0:
            send(held(0, across, c), 1, across, c, f_send.at[1, c], group_at(1))

    def to_peer(k, s, sem, who):
        copy = pltpu.make_async_remote_copy(
            src_ref=block(k, s), dst_ref=block(k, s), send_sem=sem, recv_sem=recv.at[k * 8 + s, 0],
            device_id=who, device_id_type=MESH,
        )
        copy.start()
        started.append(copy)

    def to_mate(k, s, n):
        to_peer(k, s, m_send.at[k, n], near(mate))

    def side(k, s, n):
        if k == 0:
            for c in range(parts):
                arrived(k, s, c)
        else:
            by_mate(k, s)
        to_mate(k, s, n)

    def by_mate(k, s):
        pltpu.make_async_remote_copy(
            src_ref=block(k, s), dst_ref=block(k, s), send_sem=m_send.at[k, 0], recv_sem=recv.at[k * 8 + s, 0],
            device_id=near(mate), device_id_type=MESH,
        ).wait_recv()

    def one_block(k, s):
        cross_block(wide, got, cross, k, s)

    def several(k, start, count, waiting=False):
        def one(n, carry):
            s = lax.rem(start + 2 * n, 8)
            if waiting:
                by_mate(k, s)
            cross_block(wide, got, cross, k, s)
            return carry
        lax.fori_loop(0, count, one, 0)

    def pack(k):
        rows = pl.ds(288 * k, 288)
        for t in range(TILES):
            for h in range(2):
                column = 256 * t + 128 * h
                lhs[rows, column:column + 128] = cross[pl.ds(STEP * t + 576 * h + 288 * k, 288), :].astype(bf16)

    def product(k, n):
        part = jnp.dot(lhs[pl.ds(288 * k, 288), :], table[:, 256 * n:256 * n + 256], preferred_element_type=f32)
        part = part * kept[k].astype(f32)
        for h in range(2):
            out_ref[pl.ds((2 * n + h) * 2 + k, 288, stride=16), :] = part[:, 128 * h:128 * h + 128]

    for c in range(parts):
        send(own_ref.at[pl.ds(c * rows, rows), :], 0, sta, c, y_send.at[0, c], group_at(1))
    for copy in small[5:]:
        copy.wait()
    base, offset, tables = lag_groups(bands, quick_ref)
    for t in range(8):
        lag_tile(t, base, offset, tables, slow_ref, table)
    for c in range(parts):
        own_column(0, c)
    to_mate(0, sta, 0)
    for c in range(parts):
        own_column(1, c)
    to_mate(1, sta, 0)
    several(0, sta, 1)
    for c in range(parts):
        far(0, c)
    to_mate(0, across, 3)
    side(0, left_peer, 1)
    side(0, right, 2)
    several(0, lax.rem(sta + 2, 8), 3)
    for d in range(4):
        by_mate(0, lax.rem(mate + 2 * d, 8))
    several(0, mate, 4)
    pack(0)
    for n in range(2):
        product(0, n)
    side(1, left_peer, 1)
    side(1, right, 2)
    for c in range(parts):
        far(1, c)
    to_mate(1, across, 3)
    product(0, 2)
    one_block(1, sta)
    one_block(1, left_peer)
    product(0, 3)
    one_block(1, right)
    one_block(1, across)
    several(1, lax.rem(mate + 6, 8), 3, True)
    for copy in started:
        copy.wait_send()
    several(1, lax.rem(mate + 4, 8), 1, True)
    pack(1)
    for n in range(4):
        product(1, n)


def vmem():
    return pl.BlockSpec(memory_space=pltpu.VMEM)


def body(records, fir_taps, band_bins, station_live, block_live):
    twiddle, second, slow, quick = constant_tables()
    f32, bf16 = jnp.float32, jnp.bfloat16
    x = jnp.transpose(records, (0, 2, 1, 3)).reshape(6, 4, -1)
    parts = 2
    dma = pltpu.SemaphoreType.DMA
    out = pl.pallas_call(
        functools.partial(whole_kernel, parts),
        out_shape=jax.ShapeDtypeStruct((288 * 16, 128), f32),
        in_specs=[pl.BlockSpec(memory_space=pltpu.HBM)] * 9,
        out_specs=vmem(),
        scratch_shapes=[
            pltpu.SMEM((2, 4), jnp.int32),
            pltpu.SMEM((2,), jnp.int32),
            pltpu.SMEM((64,), f32),
            pltpu.SMEM((2,), jnp.int32),
            pltpu.VMEM(twiddle.shape, f32),
            pltpu.VMEM(second.shape, f32),
            pltpu.VMEM(slow.shape, f32),
            pltpu.VMEM(quick.shape, f32),
            dma((8,)),
            pltpu.VMEM((6, 4, 16384), bf16),
            pltpu.VMEM((WINDOW, FRAMES), f32),
            pltpu.VMEM((ROWS * SPLIT, WINDOW), bf16),
            pltpu.VMEM((ROWS * SPLIT, FRAMES), f32),
            pltpu.VMEM((ROWS * TILES, 1024), f32),
            pltpu.VMEM((ROWS * 16, 128), f32),
            pltpu.VMEM((1024, 512), bf16),
            pltpu.VMEM((ROWS * 16, 128), bf16),
            pltpu.VMEM((16, ROWS * 16, 128), bf16),
            pltpu.VMEM((STEP * TILES, 128), f32),
            pltpu.VMEM((576, 2048), bf16),
            pltpu.VMEM((2048, 1024), bf16),
            dma((6,)),
            dma((2, parts)),
            dma((2, 2, parts)),
            dma((2, parts)),
            dma((2, 4)),
            dma((16, parts)),
        ],
        compiler_params=pltpu.CompilerParams(collective_id=0, has_side_effects=True, vmem_limit_bytes=VMEM_LIMIT),
        name="whole",
    )(*[
        pltpu.with_memory_space_constraint(operand, pltpu.HBM)
        for operand in (
            jnp.transpose(band_bins), station_live, fir_taps, block_live, x,
            jnp.asarray(twiddle), jnp.asarray(second), jnp.asarray(slow), jnp.asarray(quick),
        )
    ])
    out = out.reshape(288, 8, 2, 128)
    return jnp.transpose(out, (0, 2, 1, 3)).reshape(288, 2, 1024)


def solution(mesh):
    in_specs = (
        P(("section", "grp", "sta"), None, None, None),
        P(),
        P(),
        P(("section", "grp", "sta")),
        P(("section", "grp")),
    )
    out_specs = P("sta", ("section", "grp"), None)
    return jax.shard_map(body, mesh=mesh, in_specs=in_specs, out_specs=out_specs, check_vma=False)
```

```python
import functools
import math

import jax
import jax.numpy as jnp
import numpy as np
from jax import lax
from jax.experimental import pallas as pl
from jax.experimental.pallas import tpu as pltpu
from jax.sharding import PartitionSpec as P

ROWS = 24
FRAMES = 128
SPLIT = 32
WINDOW = 640
TILES = 8
STEP = 1160
MESH = pl.DeviceIdType.MESH
VMEM_LIMIT = 40 * 1024 * 1024
HIGHEST = lax.Precision.HIGHEST


def constant_tables():
    i = np.arange(128)
    k = np.arange(32)[:, None]
    turn = 2.0 * np.pi / 4096
    twiddle = np.concatenate([np.cos(turn * k * i), -np.sin(turn * k * i)], 0).astype(np.float32)
    q = np.arange(64)
    fine = 2.0 * np.pi / 128 * (i[:, None] * q[None, :] % 128)
    second = np.concatenate([np.cos(fine), np.sin(fine)], 0).astype(np.float32)
    lag = np.arange(1024) - 512
    slow = turn * (k * lag[None, :] % 4096)
    lag_slow = np.concatenate([np.cos(slow), np.sin(slow)], 0).astype(np.float32)
    quick = np.zeros((128, 256))
    angle = 2.0 * np.pi / 128 * (q[:, None] * i[None, :] % 128)
    quick[:64, :128] = np.cos(angle)
    quick[:64, 128:] = np.sin(angle)
    return twiddle, second, lag_slow, quick.astype(np.float32)


def real_fft(values):
    n = len(values)
    if n == 2:
        return [(values[0] + values[1], None), (values[0] - values[1], None)]
    even = real_fft(values[0::2])
    odd = real_fft(values[1::2])
    result = [None] * (n // 2 + 1)
    for k in range(n // 4 + 1):
        er, ei = even[k]
        orr, oi = odd[k]
        c, s = math.cos(2 * math.pi * k / n), math.sin(2 * math.pi * k / n)
        if k == 0:
            tr, ti = orr, oi
        elif 4 * k == n:
            tr, ti = oi, -orr
        elif oi is None:
            tr, ti = orr * c, orr * (-s)
        else:
            tr, ti = orr * c + oi * s, oi * c - orr * s
        def plus(a, b):
            return b if a is None else a if b is None else a + b
        def minus(a, b):
            return (None if b is None else -b) if a is None else a if b is None else a - b
        result[k] = (plus(er, tr), plus(ei, ti))
        if n // 2 - k != k:
            low = minus(ti, ei)
            result[n // 2 - k] = (minus(er, tr), low)
    return result


def filter_weights(taps, band_scr):
    f32, bf16 = jnp.float32, jnp.bfloat16
    a_index = lax.broadcasted_iota(jnp.int32, (WINDOW // 4, FRAMES), 0)
    o_index = lax.broadcasted_iota(jnp.int32, (WINDOW // 4, FRAMES), 1)
    lead = o_index - a_index + 32
    pieces = [jnp.zeros((WINDOW // 4, FRAMES), f32)] * 4
    for d in range(17):
        here = lead == d
        for b in range(4):
            if 0 <= 4 * d - b < 64:
                pieces[b] = jnp.where(here, taps[4 * d - b], pieces[b])
    for b in range(4):
        band_scr[pl.ds(b, WINDOW // 4, stride=4), :] = pieces[b]
    band = band_scr[...]
    high = band.astype(bf16)
    low = (band - high.astype(f32)).astype(bf16)
    return jnp.concatenate([high, low], axis=1)


def by_band(index, values):
    result = jnp.full(index.shape, values[3], jnp.int32)
    for b in range(3):
        result = jnp.where(index == b, values[b], result)
    return result


def band_edges(bands):
    first = [bands[0, b] for b in range(4)]
    last = [bands[1, b] for b in range(4)]
    return first, last, [s // 32 for s in first], [s % 32 for s in first]


def second_stage(bands, second_ref, w2):
    f32, bf16 = jnp.float32, jnp.bfloat16
    _, _, coarse, _ = band_edges(bands)
    q = lax.broadcasted_iota(jnp.int32, (64, 128), 0)
    lane = lax.broadcasted_iota(jnp.int32, (64, 128), 1)
    base = by_band(lane % 32 // 8, coarse) + lane % 8
    lane128 = lax.broadcasted_iota(jnp.int32, (128, 128), 1)
    for late in range(2):
        pick = jnp.where(q == base + late, 1.0, 0.0).astype(bf16)
        chosen = jnp.dot(second_ref[...].astype(bf16), pick, preferred_element_type=f32)
        for kk in range(4):
            mine = lane128 // 32 == kk
            c = jnp.where(mine, chosen[:128], 0.0)
            s = jnp.where(mine, chosen[128:], 0.0)
            top, under = pl.ds(256 * kk, 128), pl.ds(256 * kk + 128, 128)
            re, im = slice(256 * late, 256 * late + 128), slice(256 * late + 128, 256 * late + 256)
            w2[top, re] = c.astype(bf16)
            w2[top, im] = (-s).astype(bf16)
            w2[under, re] = s.astype(bf16)
            w2[under, im] = c.astype(bf16)


def transform(chunk, dec, tw_ref, lhs2):
    values = [dec[pl.ds(256 * chunk + 8 * j, 8), :] for j in range(SPLIT)]
    freq = real_fft(values)
    for k1 in range(32):
        ar, ai = freq[k1] if k1 <= 16 else freq[32 - k1]
        c = tw_ref[pl.ds(k1, 1), :]
        s = tw_ref[pl.ds(32 + k1, 1), :]
        if ai is None:
            br, bi = ar * c, ar * s
        elif k1 <= 16:
            br, bi = ar * c - ai * s, ar * s + ai * c
        else:
            br, bi = ar * c + ai * s, ar * s - ai * c
        rows = pl.ds((k1 // 4) * ROWS + 8 * chunk, 8)
        column = (k1 % 4) * 256
        lhs2[rows, column:column + 128] = br
        lhs2[rows, column + 128:column + 256] = bi


def whiten_slots(bands, live, y, wide):
    f32 = jnp.float32
    first, last, coarse, fine = band_edges(bands)
    slot = lax.broadcasted_iota(jnp.int32, (1, 128), 1)
    owner = slot % 32 // 8
    base = by_band(owner, coarse) + slot % 8
    offset = by_band(owner, fine)
    re, im, inside, counted = [], [], [], []
    for t in range(TILES):
        k1 = 4 * t + slot // 32
        late = k1 < offset
        bins = k1 + 32 * (base + jnp.where(late, 1, 0))
        rows = slice(ROWS * t, ROWS * t + ROWS)
        re.append(jnp.where(late, y[rows, 256:384], y[rows, 0:128]))
        im.append(jnp.where(late, y[rows, 384:512], y[rows, 128:256]))
        within = [(bins >= first[b]) & (bins < last[b]) for b in range(4)]
        inside.append(within)
        own = within[0] & (owner == 0)
        for b in range(1, 4):
            mine = within[b] & (owner == b)
            for earlier in range(b):
                mine = mine & jnp.logical_not(within[earlier])
            own = own | mine
        counted.append(own)
    station = lax.broadcasted_iota(jnp.int32, (ROWS, 1), 0)
    alive = jnp.where(station < 12, live[0].astype(f32), live[1].astype(f32))
    gains = [jnp.zeros((ROWS, 128), f32)] * TILES
    for b in range(4):
        total = jnp.zeros((ROWS, 128), f32)
        for t in range(TILES):
            power = re[t] * re[t] + im[t] * im[t]
            total = total + jnp.where(inside[t][b] & (owner == b), power, 0.0)
        width = (last[b] - first[b]).astype(f32)
        energy = jnp.sum(total, axis=1, keepdims=True) / width
        scale = lax.rsqrt(energy + 1e-06) * alive
        for t in range(TILES):
            gains[t] = gains[t] + jnp.where(inside[t][b], scale, 0.0)
    for t in range(TILES):
        gain = jnp.where(counted[t], gains[t], 0.0)
        wide[pl.ds(t, ROWS, stride=16), :] = re[t] * gain
        wide[pl.ds(8 + t, ROWS, stride=16), :] = im[t] * gain


def lag_groups(bands, quick_ref):
    f32 = jnp.float32
    _, _, coarse, fine = band_edges(bands)
    g = lax.broadcasted_iota(jnp.int32, (32, 128), 0)
    q = lax.broadcasted_iota(jnp.int32, (32, 128), 1)
    base = by_band(g // 8, coarse) + g % 8
    offset = by_band(g // 8, fine)
    tables = []
    for late in range(2):
        pick = jnp.where(q == base + late, 1.0, 0.0).astype(f32)
        quick = jnp.dot(pick, quick_ref[...], precision=HIGHEST, preferred_element_type=f32)
        quick = quick * f32(1.0 / math.sqrt(2048))
        tables.append((quick[:, :128], quick[:, 128:]))
    return base, offset, tables


def lag_tile(t, base, offset, tables, slow_ref, table):
    bf16 = jnp.bfloat16
    for kk in range(4):
        k1 = 4 * t + kk
        late = k1 < offset
        qc = jnp.where(late, tables[1][0], tables[0][0])
        qs = jnp.where(late, tables[1][1], tables[0][1])
        if k1 == 0:
            half = jnp.where(base + jnp.where(late, 1, 0) == 0, 0.5, 1.0)
            qc, qs = qc * half, qs * half
        row = 256 * t + 32 * kk
        for n in range(8):
            lanes = slice(128 * n, 128 * n + 128)
            sc = slow_ref[pl.ds(k1, 1), lanes]
            ss = slow_ref[pl.ds(32 + k1, 1), lanes]
            table[pl.ds(row, 32), lanes] = (sc * qc - ss * qs).astype(bf16)
            table[pl.ds(row + 128, 32), lanes] = (-(ss * qc + sc * qs)).astype(bf16)


def cross_block(left, got, cross, k, s):
    f32 = jnp.float32
    for i2 in range(2):
        for b in range(3):
            rre, rim = [], []
            for w in range(4):
                r = got[k * 8 + s, pl.ds((i2 * 12 + b * 4 + w) * 16, 16), :].astype(f32)
                rre.append(r[0:8])
                rim.append(r[8:16])
            for ia in range(6):
                re = im = None
                for w in range(4):
                    at = (ia * 4 + w) * 16
                    lre = left[at:at + 8, :]
                    lim = left[at + 8:at + 16, :]
                    pre = lre * rre[w] + lim * rim[w]
                    pim = lim * rre[w] - lre * rim[w]
                    re = pre if re is None else re + pre
                    im = pim if im is None else im + pim
                row = k * 288 + ia * 48 + s * 6 + i2 * 3 + b
                cross[pl.ds(row, 8, stride=STEP), :] = re
                cross[pl.ds(row + 576, 8, stride=STEP), :] = im


def whole_kernel(parts, bands_any, live_any, taps_any, kept_any, x_any, tw_any, second_any, slow_any, quick_any, out_ref,
                 bands, live, taps, kept, tw_ref, second_ref, slow_ref, quick_ref, in_sem, x_in, band_scr, lhs1, dec, lhs2, wide, w2, own_ref, got, cross, lhs, table,
                 x_sem, y_send, x_send, f_send, m_send, recv):
    f32, bf16 = jnp.float32, jnp.bfloat16
    section, grp, sta = lax.axis_index("section"), lax.axis_index("grp"), lax.axis_index("sta")
    groups = 16
    r = section * groups + grp
    mate = sta + 1 - 2 * lax.rem(sta, 2)
    right, across, left_peer = [lax.rem(sta + 2 * d, 8) for d in (1, 2, 3)]

    def group_at(shift):
        g = lax.rem(r + shift + 32, 32)
        return (g // groups, lax.rem(g, groups), sta)

    def near(s):
        return (section, grp, s)

    small = [
        pltpu.make_async_copy(source, place, in_sem.at[n])
        for n, (source, place) in enumerate([
            (taps_any, taps), (bands_any, bands), (second_any, second_ref), (tw_any, tw_ref), (live_any, live),
            (quick_any, quick_ref), (slow_any, slow_ref), (kept_any, kept),
        ])
    ]
    for copy in small[:3]:
        copy.start()
    fetches = [pltpu.make_async_copy(x_any.at[n], x_in.at[n], x_sem.at[n]) for n in range(6)]
    for fetch in fetches:
        fetch.start()
    for copy in small[3:]:
        copy.start()
    barrier = pltpu.get_barrier_semaphore()
    partners = [group_at(1), group_at(-1), near(mate), near(right), near(left_peer), near(across)]
    for who in partners:
        pl.semaphore_signal(barrier, inc=1, device_id=who, device_id_type=MESH)

    small[0].wait()
    weights = filter_weights(taps, band_scr)
    small[1].wait()
    small[2].wait()
    second_stage(bands, second_ref, w2)
    small[3].wait()
    small[4].wait()
    for chunk in range(3):
        fetches[2 * chunk].wait()
        fetches[2 * chunk + 1].wait()
        x = x_in[2 * chunk:2 * chunk + 2].reshape(8, -1)
        edge = jnp.concatenate([jnp.zeros((8, 128), bf16), x[:, 0:512]], axis=1)
        first = 256 * chunk
        for j in range(0, SPLIT, 2):
            head = edge if j == 0 else x[:, 512 * j - 128:512 * j + 512]
            both = jnp.concatenate([head, x[:, 512 * j + 384:512 * j + 1024]], axis=0)
            lhs1[pl.ds(first + 8 * j, 16), :] = both
        summed = jnp.dot(lhs1[pl.ds(first, 256), :], weights, preferred_element_type=f32)
        dec[pl.ds(first, 256), :] = (summed[:, :128] + summed[:, 128:]).astype(bf16).astype(f32)
        transform(chunk, dec, tw_ref, lhs2)
    y = jnp.dot(lhs2[...].astype(bf16), w2[...], preferred_element_type=f32)
    whiten_slots(bands, live, y, wide)
    own_ref[...] = wide[...].astype(bf16)

    pl.semaphore_wait(barrier, len(partners))
    rows = own_ref.shape[0] // parts
    started = []

    def held(k, s, c):
        return got.at[k * 8 + s, pl.ds(c * rows, rows), :]

    def send(src, k, s, c, sem, who):
        copy = pltpu.make_async_remote_copy(
            src_ref=src, dst_ref=held(k, s, c), send_sem=sem, recv_sem=recv.at[k * 8 + s, c],
            device_id=who, device_id_type=MESH,
        )
        copy.start()
        started.append(copy)

    def arrived(k, s, c):
        pltpu.make_async_remote_copy(
            src_ref=held(k, s, c), dst_ref=held(k, s, c), send_sem=y_send.at[0, 0],
            recv_sem=recv.at[k * 8 + s, c], device_id=near(mate), device_id_type=MESH,
        ).wait_recv()

    def block(k, s):
        return got.at[k * 8 + s]

    def own_column(k, c):
        arrived(k, sta, c)
        if k == 0:
            send(held(0, sta, c), 0, sta, c, f_send.at[0, c], near(across))
            send(held(0, sta, c), 1, sta, c, y_send.at[1, c], group_at(1))
            send(held(k, sta, c), k, sta, c, x_send.at[k, 0, c], near(right))
            send(held(k, sta, c), k, sta, c, x_send.at[k, 1, c], near(left_peer))
        elif c == parts - 1:
            to_peer(1, sta, x_send.at[1, 0, 0], near(right))
            to_peer(1, sta, x_send.at[1, 1, 0], near(left_peer))

    def far(k, c):
        arrived(k, across, c)
        if k == 0:
            send(held(0, across, c), 1, across, c, f_send.at[1, c], group_at(1))

    def to_peer(k, s, sem, who):
        copy = pltpu.make_async_remote_copy(
            src_ref=block(k, s), dst_ref=block(k, s), send_sem=sem, recv_sem=recv.at[k * 8 + s, 0],
            device_id=who, device_id_type=MESH,
        )
        copy.start()
        started.append(copy)

    def to_mate(k, s, n):
        to_peer(k, s, m_send.at[k, n], near(mate))

    def side(k, s, n):
        if k == 0:
            for c in range(parts):
                arrived(k, s, c)
        else:
            by_mate(k, s)
        to_mate(k, s, n)

    def by_mate(k, s):
        pltpu.make_async_remote_copy(
            src_ref=block(k, s), dst_ref=block(k, s), send_sem=m_send.at[k, 0], recv_sem=recv.at[k * 8 + s, 0],
            device_id=near(mate), device_id_type=MESH,
        ).wait_recv()

    def one_block(k, s):
        cross_block(wide, got, cross, k, s)

    def several(k, start, count, waiting=False):
        for n in range(count):
            s = lax.rem(start + 2 * n, 8)
            if waiting:
                by_mate(k, s)
            cross_block(wide, got, cross, k, s)

    def pack(k):
        rows = pl.ds(288 * k, 288)
        for t in range(TILES):
            for h in range(2):
                column = 256 * t + 128 * h
                lhs[rows, column:column + 128] = cross[pl.ds(STEP * t + 576 * h + 288 * k, 288), :].astype(bf16)

    def product(k, n):
        part = jnp.dot(lhs[pl.ds(288 * k, 288), :], table[:, 256 * n:256 * n + 256], preferred_element_type=f32)
        part = part * kept[k].astype(f32)
        for h in range(2):
            out_ref[pl.ds((2 * n + h) * 2 + k, 288, stride=16), :] = part[:, 128 * h:128 * h + 128]

    for c in range(parts):
        send(own_ref.at[pl.ds(c * rows, rows), :], 0, sta, c, y_send.at[0, c], group_at(1))
    for copy in small[5:]:
        copy.wait()
    base, offset, tables = lag_groups(bands, quick_ref)
    for t in range(8):
        lag_tile(t, base, offset, tables, slow_ref, table)
    for c in range(parts):
        own_column(0, c)
    to_mate(0, sta, 0)
    for c in range(parts):
        own_column(1, c)
    to_mate(1, sta, 0)
    several(0, sta, 1)
    for c in range(parts):
        far(0, c)
    to_mate(0, across, 3)
    side(0, left_peer, 1)
    side(0, right, 2)
    several(0, lax.rem(sta + 2, 8), 3)
    for d in range(4):
        by_mate(0, lax.rem(mate + 2 * d, 8))
    several(0, mate, 4)
    pack(0)
    for n in range(2):
        product(0, n)
    side(1, left_peer, 1)
    side(1, right, 2)
    for c in range(parts):
        far(1, c)
    to_mate(1, across, 3)
    product(0, 2)
    one_block(1, sta)
    one_block(1, left_peer)
    product(0, 3)
    one_block(1, right)
    one_block(1, across)
    several(1, lax.rem(mate + 6, 8), 3, True)
    for copy in started:
        copy.wait_send()
    several(1, lax.rem(mate + 4, 8), 1, True)
    pack(1)
    for n in range(4):
        product(1, n)


def vmem():
    return pl.BlockSpec(memory_space=pltpu.VMEM)


def body(records, fir_taps, band_bins, station_live, block_live):
    twiddle, second, slow, quick = constant_tables()
    f32, bf16 = jnp.float32, jnp.bfloat16
    x = jnp.transpose(records, (0, 2, 1, 3)).reshape(6, 4, -1)
    parts = 2
    dma = pltpu.SemaphoreType.DMA
    out = pl.pallas_call(
        functools.partial(whole_kernel, parts),
        out_shape=jax.ShapeDtypeStruct((288 * 16, 128), f32),
        in_specs=[pl.BlockSpec(memory_space=pltpu.HBM)] * 9,
        out_specs=vmem(),
        scratch_shapes=[
            pltpu.SMEM((2, 4), jnp.int32),
            pltpu.SMEM((2,), jnp.int32),
            pltpu.SMEM((64,), f32),
            pltpu.SMEM((2,), jnp.int32),
            pltpu.VMEM(twiddle.shape, f32),
            pltpu.VMEM(second.shape, f32),
            pltpu.VMEM(slow.shape, f32),
            pltpu.VMEM(quick.shape, f32),
            dma((8,)),
            pltpu.VMEM((6, 4, 16384), bf16),
            pltpu.VMEM((WINDOW, FRAMES), f32),
            pltpu.VMEM((ROWS * SPLIT, WINDOW), bf16),
            pltpu.VMEM((ROWS * SPLIT, FRAMES), f32),
            pltpu.VMEM((ROWS * TILES, 1024), f32),
            pltpu.VMEM((ROWS * 16, 128), f32),
            pltpu.VMEM((1024, 512), bf16),
            pltpu.VMEM((ROWS * 16, 128), bf16),
            pltpu.VMEM((16, ROWS * 16, 128), bf16),
            pltpu.VMEM((STEP * TILES, 128), f32),
            pltpu.VMEM((576, 2048), bf16),
            pltpu.VMEM((2048, 1024), bf16),
            dma((6,)),
            dma((2, parts)),
            dma((2, 2, parts)),
            dma((2, parts)),
            dma((2, 4)),
            dma((16, parts)),
        ],
        compiler_params=pltpu.CompilerParams(collective_id=0, has_side_effects=True, vmem_limit_bytes=VMEM_LIMIT),
        name="whole",
    )(*[
        pltpu.with_memory_space_constraint(operand, pltpu.HBM)
        for operand in (
            jnp.transpose(band_bins), station_live, fir_taps, block_live, x,
            jnp.asarray(twiddle), jnp.asarray(second), jnp.asarray(slow), jnp.asarray(quick),
        )
    ])
    out = out.reshape(288, 8, 2, 128)
    return jnp.transpose(out, (0, 2, 1, 3)).reshape(288, 2, 1024)


def solution(mesh):
    in_specs = (
        P(("section", "grp", "sta"), None, None, None),
        P(),
        P(),
        P(("section", "grp", "sta")),
        P(("section", "grp")),
    )
    out_specs = P("sta", ("section", "grp"), None)
    return jax.shard_map(body, mesh=mesh, in_specs=in_specs, out_specs=out_specs, check_vma=False)
```

```python
import functools
import math

import jax
import jax.numpy as jnp
import numpy as np
from jax import lax
from jax.experimental import pallas as pl
from jax.experimental.pallas import tpu as pltpu
from jax.sharding import PartitionSpec as P

ROWS = 24
FRAMES = 128
SPLIT = 32
WINDOW = 640
TILES = 8
STEP = 1160
MESH = pl.DeviceIdType.MESH
VMEM_LIMIT = 40 * 1024 * 1024
HIGHEST = lax.Precision.HIGHEST


def constant_tables():
    i = np.arange(128)
    k = np.arange(32)[:, None]
    turn = 2.0 * np.pi / 4096
    twiddle = np.concatenate([np.cos(turn * k * i), -np.sin(turn * k * i)], 0).astype(np.float32)
    q = np.arange(64)
    fine = 2.0 * np.pi / 128 * (i[:, None] * q[None, :] % 128)
    second = np.concatenate([np.cos(fine), np.sin(fine)], 0).astype(np.float32)
    lag = np.arange(1024) - 512
    slow = turn * (k * lag[None, :] % 4096)
    lag_slow = np.concatenate([np.cos(slow), np.sin(slow)], 0).astype(np.float32)
    quick = np.zeros((128, 256))
    angle = 2.0 * np.pi / 128 * (q[:, None] * i[None, :] % 128)
    quick[:64, :128] = np.cos(angle)
    quick[:64, 128:] = np.sin(angle)
    return twiddle, second, lag_slow, quick.astype(np.float32)


def real_fft(values):
    n = len(values)
    if n == 2:
        return [(values[0] + values[1], None), (values[0] - values[1], None)]
    even = real_fft(values[0::2])
    odd = real_fft(values[1::2])
    result = [None] * (n // 2 + 1)
    for k in range(n // 4 + 1):
        er, ei = even[k]
        orr, oi = odd[k]
        c, s = math.cos(2 * math.pi * k / n), math.sin(2 * math.pi * k / n)
        if k == 0:
            tr, ti = orr, oi
        elif 4 * k == n:
            tr, ti = oi, -orr
        elif oi is None:
            tr, ti = orr * c, orr * (-s)
        else:
            tr, ti = orr * c + oi * s, oi * c - orr * s
        def plus(a, b):
            return b if a is None else a if b is None else a + b
        def minus(a, b):
            return (None if b is None else -b) if a is None else a if b is None else a - b
        result[k] = (plus(er, tr), plus(ei, ti))
        if n // 2 - k != k:
            low = minus(ti, ei)
            result[n // 2 - k] = (minus(er, tr), low)
    return result


def filter_weights(taps, band_scr):
    f32, bf16 = jnp.float32, jnp.bfloat16
    a_index = lax.broadcasted_iota(jnp.int32, (WINDOW // 4, FRAMES), 0)
    o_index = lax.broadcasted_iota(jnp.int32, (WINDOW // 4, FRAMES), 1)
    lead = o_index - a_index + 32
    pieces = [jnp.zeros((WINDOW // 4, FRAMES), f32)] * 4
    for d in range(17):
        here = lead == d
        for b in range(4):
            if 0 <= 4 * d - b < 64:
                pieces[b] = jnp.where(here, taps[4 * d - b], pieces[b])
    for b in range(4):
        band_scr[pl.ds(b, WINDOW // 4, stride=4), :] = pieces[b]
    band = band_scr[...]
    high = band.astype(bf16)
    low = (band - high.astype(f32)).astype(bf16)
    return jnp.concatenate([high, low], axis=1)


def by_band(index, values):
    result = jnp.full(index.shape, values[3], jnp.int32)
    for b in range(3):
        result = jnp.where(index == b, values[b], result)
    return result


def band_edges(bands):
    first = [bands[0, b] for b in range(4)]
    last = [bands[1, b] for b in range(4)]
    return first, last, [s // 32 for s in first], [s % 32 for s in first]


def second_stage(bands, second_ref, w2):
    f32, bf16 = jnp.float32, jnp.bfloat16
    _, _, coarse, _ = band_edges(bands)
    q = lax.broadcasted_iota(jnp.int32, (64, 128), 0)
    lane = lax.broadcasted_iota(jnp.int32, (64, 128), 1)
    base = by_band(lane % 32 // 8, coarse) + lane % 8
    lane128 = lax.broadcasted_iota(jnp.int32, (128, 128), 1)
    for late in range(2):
        pick = jnp.where(q == base + late, 1.0, 0.0).astype(bf16)
        chosen = jnp.dot(second_ref[...].astype(bf16), pick, preferred_element_type=f32)
        for kk in range(4):
            mine = lane128 // 32 == kk
            c = jnp.where(mine, chosen[:128], 0.0)
            s = jnp.where(mine, chosen[128:], 0.0)
            top, under = pl.ds(256 * kk, 128), pl.ds(256 * kk + 128, 128)
            re, im = slice(256 * late, 256 * late + 128), slice(256 * late + 128, 256 * late + 256)
            w2[top, re] = c.astype(bf16)
            w2[top, im] = (-s).astype(bf16)
            w2[under, re] = s.astype(bf16)
            w2[under, im] = c.astype(bf16)


def transform(chunk, dec, tw_ref, lhs2):
    values = [dec[pl.ds(256 * chunk + 8 * j, 8), :] for j in range(SPLIT)]
    freq = real_fft(values)
    for k1 in range(32):
        ar, ai = freq[k1] if k1 <= 16 else freq[32 - k1]
        c = tw_ref[pl.ds(k1, 1), :]
        s = tw_ref[pl.ds(32 + k1, 1), :]
        if ai is None:
            br, bi = ar * c, ar * s
        elif k1 <= 16:
            br, bi = ar * c - ai * s, ar * s + ai * c
        else:
            br, bi = ar * c + ai * s, ar * s - ai * c
        rows = pl.ds((k1 // 4) * ROWS + 8 * chunk, 8)
        column = (k1 % 4) * 256
        lhs2[rows, column:column + 128] = br
        lhs2[rows, column + 128:column + 256] = bi


def whiten_slots(bands, live, y, wide):
    f32 = jnp.float32
    first, last, coarse, fine = band_edges(bands)
    slot = lax.broadcasted_iota(jnp.int32, (1, 128), 1)
    owner = slot % 32 // 8
    base = by_band(owner, coarse) + slot % 8
    offset = by_band(owner, fine)
    re, im, inside, counted = [], [], [], []
    for t in range(TILES):
        k1 = 4 * t + slot // 32
        late = k1 < offset
        bins = k1 + 32 * (base + jnp.where(late, 1, 0))
        rows = slice(ROWS * t, ROWS * t + ROWS)
        re.append(jnp.where(late, y[rows, 256:384], y[rows, 0:128]))
        im.append(jnp.where(late, y[rows, 384:512], y[rows, 128:256]))
        within = [(bins >= first[b]) & (bins < last[b]) for b in range(4)]
        inside.append(within)
        own = within[0] & (owner == 0)
        for b in range(1, 4):
            mine = within[b] & (owner == b)
            for earlier in range(b):
                mine = mine & jnp.logical_not(within[earlier])
            own = own | mine
        counted.append(own)
    station = lax.broadcasted_iota(jnp.int32, (ROWS, 1), 0)
    alive = jnp.where(station < 12, live[0].astype(f32), live[1].astype(f32))
    gains = [jnp.zeros((ROWS, 128), f32)] * TILES
    for b in range(4):
        total = jnp.zeros((ROWS, 128), f32)
        for t in range(TILES):
            power = re[t] * re[t] + im[t] * im[t]
            total = total + jnp.where(inside[t][b] & (owner == b), power, 0.0)
        width = (last[b] - first[b]).astype(f32)
        energy = jnp.sum(total, axis=1, keepdims=True) / width
        scale = lax.rsqrt(energy + 1e-06) * alive
        for t in range(TILES):
            gains[t] = gains[t] + jnp.where(inside[t][b], scale, 0.0)
    for t in range(TILES):
        gain = jnp.where(counted[t], gains[t], 0.0)
        wide[pl.ds(t, ROWS, stride=16), :] = re[t] * gain
        wide[pl.ds(8 + t, ROWS, stride=16), :] = im[t] * gain


def lag_groups(bands, quick_ref):
    f32 = jnp.float32
    _, _, coarse, fine = band_edges(bands)
    g = lax.broadcasted_iota(jnp.int32, (32, 128), 0)
    q = lax.broadcasted_iota(jnp.int32, (32, 128), 1)
    base = by_band(g // 8, coarse) + g % 8
    offset = by_band(g // 8, fine)
    tables = []
    for late in range(2):
        pick = jnp.where(q == base + late, 1.0, 0.0).astype(f32)
        quick = jnp.dot(pick, quick_ref[...], precision=HIGHEST, preferred_element_type=f32)
        quick = quick * f32(1.0 / math.sqrt(2048))
        tables.append((quick[:, :128], quick[:, 128:]))
    return base, offset, tables


def lag_tile(t, base, offset, tables, slow_ref, table):
    bf16 = jnp.bfloat16
    for kk in range(4):
        k1 = 4 * t + kk
        late = k1 < offset
        qc = jnp.where(late, tables[1][0], tables[0][0])
        qs = jnp.where(late, tables[1][1], tables[0][1])
        if k1 == 0:
            half = jnp.where(base + jnp.where(late, 1, 0) == 0, 0.5, 1.0)
            qc, qs = qc * half, qs * half
        row = 256 * t + 32 * kk
        for n in range(8):
            lanes = slice(128 * n, 128 * n + 128)
            sc = slow_ref[pl.ds(k1, 1), lanes]
            ss = slow_ref[pl.ds(32 + k1, 1), lanes]
            table[pl.ds(row, 32), lanes] = (sc * qc - ss * qs).astype(bf16)
            table[pl.ds(row + 128, 32), lanes] = (-(ss * qc + sc * qs)).astype(bf16)


def cross_block(left, got, cross, k, s):
    f32 = jnp.float32
    for i2 in range(2):
        for b in range(3):
            rre, rim = [], []
            for w in range(4):
                r = got[k * 8 + s, pl.ds((i2 * 12 + b * 4 + w) * 16, 16), :].astype(f32)
                rre.append(r[0:8])
                rim.append(r[8:16])
            for ia in range(6):
                re = im = None
                for w in range(4):
                    at = (ia * 4 + w) * 16
                    lre = left[at:at + 8, :]
                    lim = left[at + 8:at + 16, :]
                    pre = lre * rre[w] + lim * rim[w]
                    pim = lim * rre[w] - lre * rim[w]
                    re = pre if re is None else re + pre
                    im = pim if im is None else im + pim
                row = k * 288 + ia * 48 + s * 6 + i2 * 3 + b
                cross[pl.ds(row, 8, stride=STEP), :] = re
                cross[pl.ds(row + 576, 8, stride=STEP), :] = im


def whole_kernel(parts, bands_any, live_any, taps_any, kept_any, x_any, tw_any, second_any, slow_any, quick_any, out_ref,
                 bands, live, taps, kept, tw_ref, second_ref, slow_ref, quick_ref, in_sem, x_in, band_scr, lhs1, dec, lhs2, wide, w2, own_ref, got, cross, lhs, table,
                 x_sem, y_send, x_send, f_send, m_send, recv):
    f32, bf16 = jnp.float32, jnp.bfloat16
    section, grp, sta = lax.axis_index("section"), lax.axis_index("grp"), lax.axis_index("sta")
    groups = 16
    r = section * groups + grp
    mate = sta + 1 - 2 * lax.rem(sta, 2)
    right, across, left_peer = [lax.rem(sta + 2 * d, 8) for d in (1, 2, 3)]

    def group_at(shift):
        g = lax.rem(r + shift + 32, 32)
        return (g // groups, lax.rem(g, groups), sta)

    def near(s):
        return (section, grp, s)

    small = [
        pltpu.make_async_copy(source, place, in_sem.at[n])
        for n, (source, place) in enumerate([
            (taps_any, taps), (bands_any, bands), (second_any, second_ref), (tw_any, tw_ref), (live_any, live),
            (quick_any, quick_ref), (slow_any, slow_ref), (kept_any, kept),
        ])
    ]
    for copy in small[:3]:
        copy.start()
    fetches = [pltpu.make_async_copy(x_any.at[n], x_in.at[n], x_sem.at[n]) for n in range(6)]
    for fetch in fetches:
        fetch.start()
    for copy in small[3:]:
        copy.start()
    barrier = pltpu.get_barrier_semaphore()
    partners = [group_at(1), group_at(-1), near(mate), near(right), near(left_peer), near(across)]
    for who in partners:
        pl.semaphore_signal(barrier, inc=1, device_id=who, device_id_type=MESH)

    small[0].wait()
    weights = filter_weights(taps, band_scr)
    small[1].wait()
    small[2].wait()
    second_stage(bands, second_ref, w2)
    small[3].wait()
    small[4].wait()
    for chunk in range(3):
        fetches[2 * chunk].wait()
        fetches[2 * chunk + 1].wait()
        x = x_in[2 * chunk:2 * chunk + 2].reshape(8, -1)
        edge = jnp.concatenate([jnp.zeros((8, 128), bf16), x[:, 0:512]], axis=1)
        first = 256 * chunk
        for j in range(0, SPLIT, 2):
            head = edge if j == 0 else x[:, 512 * j - 128:512 * j + 512]
            both = jnp.concatenate([head, x[:, 512 * j + 384:512 * j + 1024]], axis=0)
            lhs1[pl.ds(first + 8 * j, 16), :] = both
        summed = jnp.dot(lhs1[pl.ds(first, 256), :], weights, preferred_element_type=f32)
        dec[pl.ds(first, 256), :] = (summed[:, :128] + summed[:, 128:]).astype(bf16).astype(f32)
        transform(chunk, dec, tw_ref, lhs2)
    y = jnp.dot(lhs2[...].astype(bf16), w2[...], preferred_element_type=f32)
    whiten_slots(bands, live, y, wide)
    own_ref[...] = wide[...].astype(bf16)

    pl.semaphore_wait(barrier, len(partners))
    rows = own_ref.shape[0] // parts
    started = []

    def held(k, s, c):
        return got.at[k * 8 + s, pl.ds(c * rows, rows), :]

    def send(src, k, s, c, sem, who):
        copy = pltpu.make_async_remote_copy(
            src_ref=src, dst_ref=held(k, s, c), send_sem=sem, recv_sem=recv.at[k * 8 + s, c],
            device_id=who, device_id_type=MESH,
        )
        copy.start()
        started.append(copy)

    def arrived(k, s, c):
        pltpu.make_async_remote_copy(
            src_ref=held(k, s, c), dst_ref=held(k, s, c), send_sem=y_send.at[0, 0],
            recv_sem=recv.at[k * 8 + s, c], device_id=near(mate), device_id_type=MESH,
        ).wait_recv()

    def block(k, s):
        return got.at[k * 8 + s]

    def own_column(k, c):
        arrived(k, sta, c)
        if k == 0:
            send(held(0, sta, c), 1, sta, c, y_send.at[1, c], group_at(1))
            send(held(0, sta, c), 0, sta, c, f_send.at[0, c], near(across))
            send(held(k, sta, c), k, sta, c, x_send.at[k, 0, c], near(right))
            send(held(k, sta, c), k, sta, c, x_send.at[k, 1, c], near(left_peer))
        elif c == parts - 1:
            to_peer(1, sta, x_send.at[1, 0, 0], near(right))
            to_peer(1, sta, x_send.at[1, 1, 0], near(left_peer))

    def far(k, c):
        arrived(k, across, c)
        if k == 0:
            send(held(0, across, c), 1, across, c, f_send.at[1, c], group_at(1))

    def to_peer(k, s, sem, who):
        copy = pltpu.make_async_remote_copy(
            src_ref=block(k, s), dst_ref=block(k, s), send_sem=sem, recv_sem=recv.at[k * 8 + s, 0],
            device_id=who, device_id_type=MESH,
        )
        copy.start()
        started.append(copy)

    def to_mate(k, s, n):
        to_peer(k, s, m_send.at[k, n], near(mate))

    def side(k, s, n):
        if k == 0:
            for c in range(parts):
                arrived(k, s, c)
        else:
            by_mate(k, s)
        to_mate(k, s, n)

    def by_mate(k, s):
        pltpu.make_async_remote_copy(
            src_ref=block(k, s), dst_ref=block(k, s), send_sem=m_send.at[k, 0], recv_sem=recv.at[k * 8 + s, 0],
            device_id=near(mate), device_id_type=MESH,
        ).wait_recv()

    def one_block(k, s):
        cross_block(wide, got, cross, k, s)

    def several(k, start, count, waiting=False):
        for n in range(count):
            s = lax.rem(start + 2 * n, 8)
            if waiting:
                by_mate(k, s)
            cross_block(wide, got, cross, k, s)

    def pack(k):
        rows = pl.ds(288 * k, 288)
        for t in range(TILES):
            for h in range(2):
                column = 256 * t + 128 * h
                lhs[rows, column:column + 128] = cross[pl.ds(STEP * t + 576 * h + 288 * k, 288), :].astype(bf16)

    def product(k, n):
        part = jnp.dot(lhs[pl.ds(288 * k, 288), :], table[:, 256 * n:256 * n + 256], preferred_element_type=f32)
        part = part * kept[k].astype(f32)
        for h in range(2):
            out_ref[pl.ds((2 * n + h) * 2 + k, 288, stride=16), :] = part[:, 128 * h:128 * h + 128]

    for c in range(parts):
        send(own_ref.at[pl.ds(c * rows, rows), :], 0, sta, c, y_send.at[0, c], group_at(1))
    for copy in small[5:]:
        copy.wait()
    base, offset, tables = lag_groups(bands, quick_ref)
    for t in range(8):
        lag_tile(t, base, offset, tables, slow_ref, table)
    for c in range(parts):
        own_column(0, c)
    to_mate(0, sta, 0)
    for c in range(parts):
        own_column(1, c)
    to_mate(1, sta, 0)
    several(0, sta, 1)
    for c in range(parts):
        far(0, c)
    to_mate(0, across, 3)
    side(0, left_peer, 1)
    side(0, right, 2)
    several(0, lax.rem(sta + 2, 8), 3)
    for d in range(4):
        by_mate(0, lax.rem(mate + 2 * d, 8))
    several(0, mate, 4)
    pack(0)
    for n in range(2):
        product(0, n)
    side(1, left_peer, 1)
    side(1, right, 2)
    for c in range(parts):
        far(1, c)
    to_mate(1, across, 3)
    product(0, 2)
    one_block(1, sta)
    one_block(1, left_peer)
    product(0, 3)
    one_block(1, right)
    one_block(1, across)
    several(1, lax.rem(mate + 6, 8), 3, True)
    for copy in started:
        copy.wait_send()
    several(1, lax.rem(mate + 4, 8), 1, True)
    pack(1)
    for n in range(4):
        product(1, n)


def vmem():
    return pl.BlockSpec(memory_space=pltpu.VMEM)


def body(records, fir_taps, band_bins, station_live, block_live):
    twiddle, second, slow, quick = constant_tables()
    f32, bf16 = jnp.float32, jnp.bfloat16
    x = jnp.transpose(records, (0, 2, 1, 3)).reshape(6, 4, -1)
    parts = 2
    dma = pltpu.SemaphoreType.DMA
    out = pl.pallas_call(
        functools.partial(whole_kernel, parts),
        out_shape=jax.ShapeDtypeStruct((288 * 16, 128), f32),
        in_specs=[pl.BlockSpec(memory_space=pltpu.HBM)] * 9,
        out_specs=vmem(),
        scratch_shapes=[
            pltpu.SMEM((2, 4), jnp.int32),
            pltpu.SMEM((2,), jnp.int32),
            pltpu.SMEM((64,), f32),
            pltpu.SMEM((2,), jnp.int32),
            pltpu.VMEM(twiddle.shape, f32),
            pltpu.VMEM(second.shape, f32),
            pltpu.VMEM(slow.shape, f32),
            pltpu.VMEM(quick.shape, f32),
            dma((8,)),
            pltpu.VMEM((6, 4, 16384), bf16),
            pltpu.VMEM((WINDOW, FRAMES), f32),
            pltpu.VMEM((ROWS * SPLIT, WINDOW), bf16),
            pltpu.VMEM((ROWS * SPLIT, FRAMES), f32),
            pltpu.VMEM((ROWS * TILES, 1024), f32),
            pltpu.VMEM((ROWS * 16, 128), f32),
            pltpu.VMEM((1024, 512), bf16),
            pltpu.VMEM((ROWS * 16, 128), bf16),
            pltpu.VMEM((16, ROWS * 16, 128), bf16),
            pltpu.VMEM((STEP * TILES, 128), f32),
            pltpu.VMEM((576, 2048), bf16),
            pltpu.VMEM((2048, 1024), bf16),
            dma((6,)),
            dma((2, parts)),
            dma((2, 2, parts)),
            dma((2, parts)),
            dma((2, 4)),
            dma((16, parts)),
        ],
        compiler_params=pltpu.CompilerParams(collective_id=0, has_side_effects=True, vmem_limit_bytes=VMEM_LIMIT),
        name="whole",
    )(*[
        pltpu.with_memory_space_constraint(operand, pltpu.HBM)
        for operand in (
            jnp.transpose(band_bins), station_live, fir_taps, block_live, x,
            jnp.asarray(twiddle), jnp.asarray(second), jnp.asarray(slow), jnp.asarray(quick),
        )
    ])
    out = out.reshape(288, 8, 2, 128)
    return jnp.transpose(out, (0, 2, 1, 3)).reshape(288, 2, 1024)


def solution(mesh):
    in_specs = (
        P(("section", "grp", "sta"), None, None, None),
        P(),
        P(),
        P(("section", "grp", "sta")),
        P(("section", "grp")),
    )
    out_specs = P("sta", ("section", "grp"), None)
    return jax.shard_map(body, mesh=mesh, in_specs=in_specs, out_specs=out_specs, check_vma=False)
```
